32 devices in a mesh: seq: 8 (over y, x, core), head: 4 (over z).
Axes of the slice: x: 2, y: 2, z: 4, core: 2. Of those that a mesh axis runs over, the one named last changes fastest.
Arguments:
- queries: bfloat16 [4096, 8192], P('seq', 'head'), may hold values from -0.9 to 0.9
- keys: bfloat16 [4096, 8192], P('seq', 'head'), may hold values from -0.9 to 0.9
- values: bfloat16 [4096, 8192], P('seq', 'head'), may hold values from -0.9 to 0.9
- grad_out: bfloat16 [4096, 8192], P('seq', 'head'), may hold values from -0.9 to 0.9
- rates: float32 [64], P('head'), may hold values from 0.00012207031 to 0.04
- doc_lengths: int32 [8], replicated, may hold values from 1 to 3072, 4096 in all
Outputs:
- grad_queries: bfloat16 [4096, 8192], P(('seq', 'head'))
- grad_keys: bfloat16 [4096, 8192], P(('seq', 'head'))
- grad_values: bfloat16 [4096, 8192], P(('seq', 'head'))
The draws below stay inside these ranges and needn't reach their ends.
Inputs may be any that keep to these rules, and one draw needn't show every extreme that they name: `doc_lengths`: lengths of the completions in order, summing to 4096; the longest has exactly 3072 tokens.
All inputs are finite; a program needn't handle non-finite values.
Results may differ from the reference program's by a relative error of at most 0.001.
The reference program's roundings to bfloat16 on the way count: a program that leaves them out, or rounds other values in their place, can miss the bound.
Values may be sent and summed in bfloat16 or wider, within the bound.
A program may use at most 128 MiB of HBM per device.

```python
import math
import jax
import jax.numpy as jnp
import numpy as np
from jax import lax

H = 64
HD = 128
TOK_DEV = 512
DOCS = 8
TOKENS = 4096
MOST = 3072
INNER = 8192


def loud_blocks(key, salt):
    own_key = jax.random.fold_in(key, salt)
    entry_key, factor_key = jax.random.split(own_key)
    entries = jnp.clip(0.15 * jax.random.normal(entry_key, (TOKENS, INNER), jnp.float32), -0.9, 0.9)
    blocks = TOKENS // TOK_DEV
    factors = jnp.exp(-3.4 * jax.random.uniform(factor_key, (blocks, 1, 1), jnp.float32))
    shaped = entries.reshape(blocks, TOK_DEV, INNER) * factors
    return shaped.reshape(TOKENS, INNER).astype(jnp.bfloat16)


def draw_queries(key, part):
    return loud_blocks(key, 101)


def draw_keys(key, part):
    return loud_blocks(key, 202)


def draw_values(key, part):
    return loud_blocks(key, 303)


def draw_grad_out(key, part):
    return loud_blocks(key, 404)


def block_levels(key, shape, cuts, least, high):
    gain = 1.0
    for position, parts in cuts:
        draws = jax.random.uniform(jax.random.fold_in(jax.random.fold_in(key, 6), position), (parts,), jnp.float32, least / len(cuts), high / len(cuts))
        gain = gain * jnp.repeat(jnp.exp(draws), shape[position] // parts).reshape((-1,) + (1,) * (len(shape) - 1 - position))
    return gain


def split_up(count, total, reach, skew):
    portions = [(1 << 20) // math.isqrt(rank ** skew) + 1 for rank in range(2, count + 1)]
    rest, given = total - reach - (count - 1), [1] * (count - 1)
    while rest > 0:
        free = [i for i in range(count - 1) if given[i] < reach]
        mass, left = sum([portions[i] for i in free]), rest
        for i in free:
            more = min(reach - given[i], max(1, left * portions[i] // mass), rest)
            given[i] = given[i] + more
            rest = rest - more
    return np.array([reach] + given)


def ragged(key, count, total, reach, slope):
    if count == 2:
        one = jax.random.randint(key, (), max(1, total - reach), min(reach, total - 1) + 1)
        return jnp.stack([one, total - one])
    sizes = jnp.asarray(split_up(count, total, reach, slope), jnp.int32)
    twos = (count - 1) // 2
    giver, receiver = sizes[1:1 + 2 * twos:2], sizes[2:2 + 2 * twos:2]
    room = jnp.minimum(giver - 1, reach - receiver)
    passed = jax.random.randint(jax.random.fold_in(key, 1), (twos,), 0, 1 << 20) % (room + 1)
    sizes = sizes.at[1:1 + 2 * twos:2].set(giver - passed).at[2:2 + 2 * twos:2].set(receiver + passed)
    return sizes[jax.random.permutation(jax.random.fold_in(key, 2), count)]


def setup_inputs(seed: int = 0) -> dict:
    streams_of = jax.random.split(jax.random.key(seed), 7)
    queries = draw_queries(jax.random.fold_in(streams_of[6], 71), 0)
    keys = draw_keys(jax.random.fold_in(streams_of[6], 71), 0)
    values = draw_values(jax.random.fold_in(streams_of[6], 71), 0)
    grad_out = draw_grad_out(jax.random.fold_in(streams_of[6], 71), 0)
    rates = jnp.clip(jnp.exp(math.log(0.04) - 5.7920375 * jax.random.uniform(streams_of[4], (H,), jnp.float32) ** block_levels(streams_of[4], (H,), ((0, 4),), -0.2, 0.2)), 0.00012207031, 0.04)
    doc_lengths = ragged(streams_of[5], DOCS, TOKENS, MOST, 2).astype(jnp.int32)
    return dict(queries=queries, keys=keys, values=values, grad_out=grad_out, rates=rates, doc_lengths=doc_lengths)


def seg_ids(doc_lengths, positions):
    starts = jnp.cumsum(doc_lengths, dtype=jnp.int32) - doc_lengths
    inside = (starts[None, :] <= positions[:, None]).astype(jnp.int32)
    return jnp.sum(inside, axis=1, dtype=jnp.int32) - 1


def rounded(array):
    return lax.optimization_barrier(array.astype(jnp.bfloat16)).astype(jnp.float32)


def block_grads(query_rows, key_rows, value_rows, grad_rows, segment, seg_prev, seg_next, state_in, back_in, rates):
    length = query_rows.shape[0]
    offsets = jnp.arange(length, dtype=jnp.float32)
    distance = offsets[:, None] - offsets[None, :]
    allowed = (segment[:, None] == segment[None, :]) & (distance >= 0)
    decayed = jnp.where(allowed[None], jnp.exp(-rates[:, None, None] * jnp.maximum(distance, 0.0)[None]), 0.0)
    query_full = query_rows.astype(jnp.float32)
    key_full = key_rows.astype(jnp.float32)
    value_full = value_rows.astype(jnp.float32)
    grad_full = grad_rows.astype(jnp.float32)
    scores_gv = jnp.einsum("the,uhe->htu", grad_full, value_full)
    scores_qk = jnp.einsum("thd,uhd->htu", query_full, key_full)
    weights_p = rounded(decayed * scores_gv)
    weights_a = rounded(decayed * scores_qk)
    local_q = jnp.einsum("htu,uhd->thd", weights_p, key_full)
    local_k = jnp.einsum("htu,thd->uhd", weights_p, query_full)
    local_v = jnp.einsum("htu,the->uhe", weights_a, grad_full)
    factor_in = jnp.where((segment == seg_prev)[:, None], jnp.exp(-rates[None, :] * (offsets + 1.0)[:, None]), 0.0)
    factor_back = jnp.where((segment == seg_next)[:, None], jnp.exp(-rates[None, :] * (length - offsets)[:, None]), 0.0)
    state_b = rounded(state_in)
    back_b = rounded(back_in)
    outer_q = jnp.einsum("the,hde->thd", grad_full, state_b) * factor_in[:, :, None]
    outer_k = jnp.einsum("the,hde->thd", value_full, back_b) * factor_back[:, :, None]
    outer_v = jnp.einsum("thd,hde->the", key_full, back_b) * factor_back[:, :, None]
    return ((local_q + outer_q).astype(jnp.bfloat16), (local_k + outer_k).astype(jnp.bfloat16), (local_v + outer_v).astype(jnp.bfloat16))


def reference(queries, keys, values, grad_out, rates, doc_lengths):
    length = TOK_DEV
    blocks = TOKENS // TOK_DEV
    query_blk = queries.reshape(blocks, length, H, HD)
    key_blk = keys.reshape(blocks, length, H, HD)
    value_blk = values.reshape(blocks, length, H, HD)
    grad_blk = grad_out.reshape(blocks, length, H, HD)
    positions = jnp.arange(TOKENS, dtype=jnp.int32)
    segment = seg_ids(doc_lengths, positions).reshape(blocks, length)
    firsts = jnp.arange(blocks, dtype=jnp.int32) * length
    seg_prev = seg_ids(doc_lengths, firsts - 1)
    seg_next = seg_ids(doc_lengths, firsts + length)
    keep_fwd = (segment[:, -1] == seg_prev).astype(jnp.float32)
    keep_bwd = (segment[:, 0] == seg_next).astype(jnp.float32)
    decay = jnp.exp(-rates * length)
    offsets = jnp.arange(length, dtype=jnp.float32)

    def forward_step(carry, items):
        key_rows, value_rows, seg_rows, keep = items
        weight = jnp.where((seg_rows == seg_rows[-1])[:, None], jnp.exp(-rates[None, :] * (length - 1.0 - offsets)[:, None]), 0.0)
        weighted = rounded(key_rows.astype(jnp.float32) * weight[:, :, None])
        summary = jnp.einsum("uhd,uhe->hde", weighted, value_rows.astype(jnp.float32))
        return keep * decay[:, None, None] * carry + summary, carry

    def backward_step(carry, items):
        query_rows, grad_rows, seg_rows, keep = items
        weight = jnp.where((seg_rows == seg_rows[0])[:, None], jnp.exp(-rates[None, :] * offsets[:, None]), 0.0)
        weighted = rounded(query_rows.astype(jnp.float32) * weight[:, :, None])
        summary = jnp.einsum("thd,the->hde", weighted, grad_rows.astype(jnp.float32))
        return keep * decay[:, None, None] * carry + summary, carry

    zero_state = jnp.zeros((H, HD, HD), jnp.float32)
    _, states_in = lax.scan(forward_step, zero_state, (key_blk, value_blk, segment, keep_fwd))
    _, backs_in = lax.scan(backward_step, zero_state, (query_blk, grad_blk, segment, keep_bwd), reverse=True)

    def one_block(items):
        query_rows, key_rows, value_rows, grad_rows, seg_rows, prev_one, next_one, state_one, back_one = items
        return block_grads(query_rows, key_rows, value_rows, grad_rows, seg_rows, prev_one, next_one, state_one, back_one, rates)

    grad_q, grad_k, grad_v = lax.map(one_block, (query_blk, key_blk, value_blk, grad_blk, segment, seg_prev, seg_next, states_in, backs_in))
    return (grad_q.reshape(TOKENS, INNER), grad_k.reshape(TOKENS, INNER), grad_v.reshape(TOKENS, INNER))
```

```python
import functools

import jax
import jax.numpy as jnp
from jax import lax
from jax.experimental import pallas as pl
from jax.experimental.pallas import tpu as pltpu
from jax.sharding import PartitionSpec as P

MESH = pl.DeviceIdType.MESH
NEVER = 1e30
LEAD = 3


def dot(a, b, dims):
    return lax.dot_general(a, b, (dims, ((), ())), preferred_element_type=jnp.float32)


NN = ((1,), (0,))
NT = ((1,), (1,))
TN = ((0,), (0,))


def kernel(
    shards,
    groups,
    docs,
    lengths,
    rates,
    q_hbm,
    k_hbm,
    v_hbm,
    g_hbm,
    dq_hbm,
    dk_hbm,
    dv_hbm,
    rows_in,
    dist,
    row_dist,
    sums,
    gathered,
    acc,
    stage,
    land,
    gaps,
    load_sem,
    sum_send,
    sum_recv,
    out_send,
    out_recv,
    write_sem,
):
    heads, _, length, head_dim = rows_in.shape
    part = length // groups
    shard = lax.axis_index("seq")
    group = lax.axis_index("head")
    inputs = (q_hbm, k_hbm, v_hbm, g_hbm)
    outputs = (dq_hbm, dk_hbm, dv_hbm)

    def load(h):
        columns = pl.ds(pl.multiple_of(h * head_dim, head_dim), head_dim)
        return [
            pltpu.make_async_copy(ref.at[:, columns], rows_in.at[h, i], load_sem.at[h])
            for i, ref in enumerate(inputs)
        ]

    @pl.loop(0, heads)
    def _(h):
        for copy in load(h):
            copy.start()

    barrier = pltpu.get_barrier_semaphore()
    for d in range(1, shards):
        peer = lax.rem(shard + d, shards)
        pl.semaphore_signal(barrier, inc=1, device_id=(peer, group), device_id_type=MESH)
    for d in range(1, groups):
        peer = lax.rem(group + d, groups)
        pl.semaphore_signal(barrier, inc=1, device_id=(shard, peer), device_id_type=MESH)

    first = shard * length

    def starts():
        total = jnp.int32(0)
        for i in range(docs):
            yield total
            total = total + lengths[i]

    def seg(positions):
        count = -1
        for start in starts():
            count = count + jnp.where(start <= positions, 1, 0)
        return count

    seg_first = seg(first)
    seg_last = seg(first + length - 1)
    seg_prev = seg(first - 1)
    seg_next = seg(first + length)
    wide = (length, head_dim)
    offset = lax.broadcasted_iota(jnp.int32, wide, 0)
    segment = seg(first + offset)
    where = offset.astype(jnp.float32)
    row_dist[0] = jnp.where(segment == seg_last, length - 1.0 - where, NEVER)
    row_dist[1] = jnp.where(segment == seg_first, where, NEVER)
    row_dist[2] = jnp.where(segment == seg_prev, where + 1.0, NEVER)
    row_dist[3] = jnp.where(segment == seg_next, length - where, NEVER)

    def summarise(h):
        pltpu.make_async_copy(rows_in.at[h], rows_in.at[h], load_sem.at[h]).wait()
        rate = rates[h]
        weighted_k = (
            rows_in[h, 1].astype(jnp.float32) * jnp.exp(-rate * row_dist[0])
        ).astype(jnp.bfloat16)
        sums[0, h] = dot(weighted_k, rows_in[h, 2], TN)
        weighted_q = (
            rows_in[h, 0].astype(jnp.float32) * jnp.exp(-rate * row_dist[1])
        ).astype(jnp.bfloat16)
        sums[1, h] = dot(weighted_q, rows_in[h, 3], TN)

    def send_sums(h):
        for d in range(1, shards):
            peer = lax.rem(shard + d, shards)
            back = (shard + d) // shards
            pltpu.make_async_remote_copy(
                src_ref=sums.at[back, h],
                dst_ref=gathered.at[h, d - 1],
                send_sem=sum_send.at[h],
                recv_sem=sum_recv.at[h],
                device_id=(peer, group),
                device_id_type=MESH,
            ).start()

    summarise(0)
    pl.semaphore_wait(barrier, shards + groups - 2)
    send_sums(0)

    for d in range(1, shards):
        source = lax.rem(shard - d + shards, shards)
        ahead = (shard + shards - d) // shards
        same_fwd = seg((source + 1) * length - 1) == seg_prev
        same_bwd = seg(source * length) == seg_next
        gaps[0, d - 1] = jnp.where(
            jnp.logical_and(ahead == 1, same_fwd), float(length * (d - 1)), NEVER
        )
        gaps[1, d - 1] = jnp.where(
            jnp.logical_and(ahead == 0, same_bwd), float(length * (shards - d - 1)), NEVER
        )

    lead = min(LEAD, heads)
    for h in range(1, lead):
        summarise(h)
        send_sums(h)

    tile = min(256, length)
    tiles = length // tile
    across = lax.broadcasted_iota(jnp.int32, (1, length), 1)
    seg_across = seg(first + across)
    for i in range(tiles):
        down = i * tile + lax.broadcasted_iota(jnp.int32, (tile, 1), 0)
        seg_down = seg(first + down)
        gap = down - across
        dist[pl.ds(i * tile, tile), :] = jnp.where(
            jnp.logical_and(seg_down == seg_across, gap >= 0), gap.astype(jnp.float32), NEVER
        )

    order = sorted(range(1, groups), key=lambda d: abs(2 * d - groups))

    def own(h):
        columns = pl.ds(pl.multiple_of((group * heads + h) * head_dim, head_dim), head_dim)
        return [
            pltpu.make_async_copy(stage.at[h, group, c], ref.at[:, columns], write_sem)
            for c, ref in enumerate(outputs)
        ]

    def push(h, d):
        peer = lax.rem(group + d, groups)
        return pltpu.make_async_remote_copy(
            src_ref=stage.at[h, peer],
            dst_ref=land.at[d - 1, h],
            send_sem=out_send,
            recv_sem=out_recv.at[d - 1, h],
            device_id=(shard, peer),
            device_id_type=MESH,
        )

    @pl.loop(0, heads)
    def _(h):
        @pl.when(h + lead < heads)
        def _():
            summarise(h + lead)
            send_sums(h + lead)

        rate = rates[h]
        for i in range(tiles):
            rows, seen = pl.ds(i * tile, tile), (i + 1) * tile
            q, g = rows_in[h, 0, rows], rows_in[h, 3, rows]
            k, v = rows_in[h, 1, pl.ds(0, seen)], rows_in[h, 2, pl.ds(0, seen)]
            decay = jnp.exp(-rate * dist[rows, pl.ds(0, seen)])
            p = (decay * dot(g, v, NT)).astype(jnp.bfloat16)
            a = (decay * dot(q, k, NT)).astype(jnp.bfloat16)
            acc[0, rows] = dot(p, k, NN)
            dk, dv = dot(p, q, TN), dot(a, g, TN)
            if i:
                acc[1, pl.ds(0, i * tile)] += dk[: i * tile]
                acc[2, pl.ds(0, i * tile)] += dv[: i * tile]
            acc[1, rows] = dk[i * tile :]
            acc[2, rows] = dv[i * tile :]

        pltpu.make_async_copy(gathered.at[h], gathered.at[h], sum_recv.at[h]).wait()
        state = jnp.zeros((head_dim, head_dim), jnp.float32)
        back = jnp.zeros((head_dim, head_dim), jnp.float32)
        for d in range(shards - 1):
            summary = gathered[h, d]
            state += jnp.exp(jnp.full((1, head_dim), -rate * gaps[0, d])) * summary
            back += jnp.exp(jnp.full((1, head_dim), -rate * gaps[1, d])) * summary
        state = state.astype(jnp.bfloat16)
        back = back.astype(jnp.bfloat16)
        factor_in = jnp.exp(-rate * row_dist[2])
        factor_back = jnp.exp(-rate * row_dist[3])
        dq = acc[0] + dot(rows_in[h, 3], state, NT) * factor_in
        dk = acc[1] + dot(rows_in[h, 2], back, NT) * factor_back
        dv = acc[2] + dot(rows_in[h, 1], back, NN) * factor_back
        for c, total in enumerate((dq, dk, dv)):
            stage[h, :, c] = total.astype(jnp.bfloat16).reshape(groups, part, head_dim)
        for d in order:
            push(h, d).start()
        for copy in own(h):
            copy.start()

    def landed(h, d):
        source = lax.rem(group - d + groups, groups)
        columns = pl.ds(pl.multiple_of((source * heads + h) * head_dim, head_dim), head_dim)
        return [
            pltpu.make_async_copy(land.at[d - 1, h, c], ref.at[:, columns], write_sem)
            for c, ref in enumerate(outputs)
        ]

    @pl.loop(0, heads)
    def _(h):
        for d in order:
            push(h, d).wait_recv()
            for copy in landed(h, d):
                copy.start()

    @pl.loop(0, heads)
    def _(h):
        pltpu.make_async_copy(gathered.at[h], gathered.at[h], sum_send.at[h]).wait()

    pltpu.make_async_copy(land, land, out_send).wait()
    pltpu.make_async_copy(stage, stage, write_sem).wait()


def body(queries, keys, values, grad_out, rates, doc_lengths):
    length, columns = queries.shape
    heads = rates.shape[0]
    head_dim = columns // heads
    shards = lax.axis_size("seq")
    groups = lax.axis_size("head")
    part = length // groups
    docs = doc_lengths.shape[0]
    smem = pl.BlockSpec(memory_space=pltpu.SMEM)
    hbm = pl.BlockSpec(memory_space=pl.ANY)
    bf16, f32 = jnp.bfloat16, jnp.float32
    out = jax.ShapeDtypeStruct((part, groups * columns), bf16)
    return pl.pallas_call(
        functools.partial(kernel, shards, groups, docs),
        out_shape=(out, out, out),
        in_specs=[smem, smem, hbm, hbm, hbm, hbm],
        out_specs=(hbm, hbm, hbm),
        scratch_shapes=[
            pltpu.VMEM((heads, 4, length, head_dim), bf16),
            pltpu.VMEM((length, length), f32),
            pltpu.VMEM((4, length, head_dim), f32),
            pltpu.VMEM((2, heads, head_dim, head_dim), f32),
            pltpu.VMEM((heads, shards - 1, head_dim, head_dim), f32),
            pltpu.VMEM((3, length, head_dim), f32),
            pltpu.VMEM((heads, groups, 3, part, head_dim), bf16),
            pltpu.VMEM((groups - 1, heads, 3, part, head_dim), bf16),
            pltpu.SMEM((2, shards - 1), f32),
            pltpu.SemaphoreType.DMA((heads,)),
            pltpu.SemaphoreType.DMA((heads,)),
            pltpu.SemaphoreType.DMA((heads,)),
            pltpu.SemaphoreType.DMA,
            pltpu.SemaphoreType.DMA((groups - 1, heads)),
            pltpu.SemaphoreType.DMA,
        ],
        compiler_params=pltpu.CompilerParams(
            collective_id=0, has_side_effects=True, vmem_limit_bytes=48 * 1024 * 1024
        ),
        cost_estimate=pl.CostEstimate(
            flops=heads * length * (10 * length + 10 * head_dim) * head_dim,
            bytes_accessed=7 * length * columns * 2,
            transcendentals=heads * length * (length + 4 * head_dim),
        ),
    )(doc_lengths, rates, queries, keys, values, grad_out)


def solution(mesh):
    return jax.shard_map(
        body,
        mesh=mesh,
        in_specs=(
            P("seq", "head"),
            P("seq", "head"),
            P("seq", "head"),
            P("seq", "head"),
            P("head"),
            P(),
        ),
        out_specs=(P(("seq", "head"), None), P(("seq", "head"), None), P(("seq", "head"), None)),
        check_vma=False,
    )
```

```python
import functools

import jax
import jax.numpy as jnp
from jax import lax
from jax.experimental import pallas as pl
from jax.experimental.pallas import tpu as pltpu
from jax.sharding import PartitionSpec as P

MESH = pl.DeviceIdType.MESH
NEVER = 1e30
LEAD = 3
VMEM_BYTES = 62 * 1024 * 1024


def dot(a, b, dims):
    return lax.dot_general(a, b, (dims, ((), ())), preferred_element_type=jnp.float32)


NN = ((1,), (0,))
NT = ((1,), (1,))
TN = ((0,), (0,))


def kernel(
    shards,
    groups,
    docs,
    lengths_hbm,
    rates_hbm,
    q_hbm,
    k_hbm,
    v_hbm,
    g_hbm,
    land,
    lengths,
    rates,
    rows_in,
    dist,
    row_dist,
    sums,
    gathered,
    acc,
    stage,
    gaps,
    load_sem,
    sum_send,
    sum_recv,
    out_send,
    out_recv,
    small_sem,
):
    heads, _, length, head_dim = rows_in.shape
    part = length // groups
    shard = lax.axis_index("seq")
    group = lax.axis_index("head")
    inputs = (q_hbm, k_hbm, v_hbm, g_hbm)

    def load(h):
        columns = pl.ds(pl.multiple_of(h * head_dim, head_dim), head_dim)
        return [
            pltpu.make_async_copy(ref.at[:, columns], rows_in.at[h, i], load_sem.at[h])
            for i, ref in enumerate(inputs)
        ]

    small = [
        pltpu.make_async_copy(lengths_hbm, lengths, small_sem.at[0]),
        pltpu.make_async_copy(rates_hbm, rates, small_sem.at[1]),
    ]
    for copy in small + load(0):
        copy.start()

    barrier = pltpu.get_barrier_semaphore()
    for d in range(1, shards):
        peer = lax.rem(shard + d, shards)
        pl.semaphore_signal(barrier, inc=1, device_id=(peer, group), device_id_type=MESH)
    for d in range(1, groups):
        peer = lax.rem(group + d, groups)
        pl.semaphore_signal(barrier, inc=1, device_id=(shard, peer), device_id_type=MESH)

    first = shard * length
    for copy in small:
        copy.wait()

    def starts():
        total = jnp.int32(0)
        for i in range(docs):
            yield total
            total = total + lengths[i]

    def seg(positions):
        count = -1
        for start in starts():
            count = count + jnp.where(start <= positions, 1, 0)
        return count

    seg_first = seg(first)
    seg_last = seg(first + length - 1)
    seg_prev = seg(first - 1)
    seg_next = seg(first + length)
    wide = (length, head_dim)
    offset = lax.broadcasted_iota(jnp.int32, wide, 0)
    segment = seg(first + offset)
    where = offset.astype(jnp.float32)
    row_dist[0] = jnp.where(segment == seg_last, length - 1.0 - where, NEVER)
    row_dist[1] = jnp.where(segment == seg_first, where, NEVER)

    def summarise(h):
        pltpu.make_async_copy(rows_in.at[h], rows_in.at[h], load_sem.at[h]).wait()
        rate = rates[h]
        weighted_k = (
            rows_in[h, 1].astype(jnp.float32) * jnp.exp(-rate * row_dist[0])
        ).astype(jnp.bfloat16)
        sums[0, h] = dot(weighted_k, rows_in[h, 2], TN)
        weighted_q = (
            rows_in[h, 0].astype(jnp.float32) * jnp.exp(-rate * row_dist[1])
        ).astype(jnp.bfloat16)
        sums[1, h] = dot(weighted_q, rows_in[h, 3], TN)

    def send_sums(h):
        for d in range(1, shards):
            peer = lax.rem(shard + d, shards)
            back = (shard + d) // shards
            pltpu.make_async_remote_copy(
                src_ref=sums.at[back, h],
                dst_ref=gathered.at[h, d - 1],
                send_sem=sum_send.at[h],
                recv_sem=sum_recv.at[h],
                device_id=(peer, group),
                device_id_type=MESH,
            ).start()

    summarise(0)
    pl.semaphore_wait(barrier, shards + groups - 2)
    send_sums(0)

    @pl.loop(1, heads)
    def _(h):
        for copy in load(h):
            copy.start()

    row_dist[2] = jnp.where(segment == seg_prev, where + 1.0, NEVER)
    row_dist[3] = jnp.where(segment == seg_next, length - where, NEVER)

    for d in range(1, shards):
        source = lax.rem(shard - d + shards, shards)
        ahead = (shard + shards - d) // shards
        same_fwd = seg((source + 1) * length - 1) == seg_prev
        same_bwd = seg(source * length) == seg_next
        gaps[0, d - 1] = jnp.where(
            jnp.logical_and(ahead == 1, same_fwd), float(length * (d - 1)), NEVER
        )
        gaps[1, d - 1] = jnp.where(
            jnp.logical_and(ahead == 0, same_bwd), float(length * (shards - d - 1)), NEVER
        )

    lead = min(LEAD, heads)
    for h in range(1, lead):
        summarise(h)
        send_sums(h)

    tile = min(256, length)
    tiles = length // tile
    across = lax.broadcasted_iota(jnp.int32, (1, length), 1)
    seg_across = seg(first + across)
    for i in range(tiles):
        down = i * tile + lax.broadcasted_iota(jnp.int32, (tile, 1), 0)
        seg_down = seg(first + down)
        gap = down - across
        dist[pl.ds(i * tile, tile), :] = jnp.where(
            jnp.logical_and(seg_down == seg_across, gap >= 0), gap.astype(jnp.float32), NEVER
        )

    order = sorted(range(1, groups), key=lambda d: abs(2 * d - groups))

    def columns_of(source, h):
        return pl.ds(pl.multiple_of((source * heads + h) * head_dim, head_dim), head_dim)

    def push(h, d):
        peer = lax.rem(group + d, groups)
        return pltpu.make_async_remote_copy(
            src_ref=stage.at[h, peer],
            dst_ref=land.at[:, :, columns_of(group, h)],
            send_sem=out_send,
            recv_sem=out_recv.at[d - 1, h],
            device_id=(shard, peer),
            device_id_type=MESH,
        )

    @pl.loop(0, heads)
    def _(h):
        @pl.when(h + lead < heads)
        def _():
            summarise(h + lead)
            send_sums(h + lead)

        rate = rates[h]
        for i in range(tiles):
            rows, seen = pl.ds(i * tile, tile), (i + 1) * tile
            q, g = rows_in[h, 0, rows], rows_in[h, 3, rows]
            k, v = rows_in[h, 1, pl.ds(0, seen)], rows_in[h, 2, pl.ds(0, seen)]
            decay = jnp.exp(-rate * dist[rows, pl.ds(0, seen)])
            p = (decay * dot(g, v, NT)).astype(jnp.bfloat16)
            a = (decay * dot(q, k, NT)).astype(jnp.bfloat16)
            acc[0, rows] = dot(p, k, NN)
            dk, dv = dot(p, q, TN), dot(a, g, TN)
            if i:
                acc[1, pl.ds(0, i * tile)] += dk[: i * tile]
                acc[2, pl.ds(0, i * tile)] += dv[: i * tile]
            acc[1, rows] = dk[i * tile :]
            acc[2, rows] = dv[i * tile :]

        pltpu.make_async_copy(gathered.at[h], gathered.at[h], sum_recv.at[h]).wait()
        state = jnp.zeros((head_dim, head_dim), jnp.float32)
        back = jnp.zeros((head_dim, head_dim), jnp.float32)
        for d in range(shards - 1):
            summary = gathered[h, d]
            state += jnp.exp(jnp.full((1, head_dim), -rate * gaps[0, d])) * summary
            back += jnp.exp(jnp.full((1, head_dim), -rate * gaps[1, d])) * summary
        state = state.astype(jnp.bfloat16)
        back = back.astype(jnp.bfloat16)
        factor_in = jnp.exp(-rate * row_dist[2])
        factor_back = jnp.exp(-rate * row_dist[3])
        dq = acc[0] + dot(rows_in[h, 3], state, NT) * factor_in
        dk = acc[1] + dot(rows_in[h, 2], back, NT) * factor_back
        dv = acc[2] + dot(rows_in[h, 1], back, NN) * factor_back
        for c, total in enumerate((dq, dk, dv)):
            stage[h, :, c] = total.astype(jnp.bfloat16).reshape(groups, part, head_dim)
        for d in order:
            push(h, d).start()
        land[:, :, columns_of(group, h)] = stage[h, group]

    @pl.loop(0, heads)
    def _(h):
        for d in order:
            push(h, d).wait_recv()

    @pl.loop(0, heads)
    def _(h):
        pltpu.make_async_copy(gathered.at[h], gathered.at[h], sum_send.at[h]).wait()

    sent = stage.at[:, pl.ds(0, groups - 1)]
    pltpu.make_async_copy(sent, sent, out_send).wait()


def write_out(land, dq_hbm, dk_hbm, dv_hbm, write_sem):
    columns = land.shape[2]
    pieces = 4
    width = columns // pieces
    copies = []
    for c, ref in enumerate((dq_hbm, dk_hbm, dv_hbm)):
        for i in range(pieces):
            piece = pl.ds(i * width, width)
            copies.append(
                pltpu.make_async_copy(
                    land.at[c, :, piece], ref.at[:, piece], write_sem.at[c * pieces + i]
                )
            )
    for copy in copies:
        copy.start()
    for copy in copies:
        copy.wait()


def body(queries, keys, values, grad_out, rates, doc_lengths):
    length, columns = queries.shape
    heads = rates.shape[0]
    head_dim = columns // heads
    shards = lax.axis_size("seq")
    groups = lax.axis_size("head")
    part = length // groups
    docs = doc_lengths.shape[0]
    hbm = pl.BlockSpec(memory_space=pltpu.HBM)
    vmem = pl.BlockSpec(memory_space=pltpu.VMEM)
    bf16, f32 = jnp.bfloat16, jnp.float32
    landed = pl.pallas_call(
        functools.partial(kernel, shards, groups, docs),
        out_shape=pltpu.VMEM((3, part, groups * columns), bf16),
        in_specs=[hbm] * 6,
        out_specs=vmem,
        scratch_shapes=[
            pltpu.SMEM(doc_lengths.shape, jnp.int32),
            pltpu.SMEM(rates.shape, f32),
            pltpu.VMEM((heads, 4, length, head_dim), bf16),
            pltpu.VMEM((length, length), f32),
            pltpu.VMEM((4, length, head_dim), f32),
            pltpu.VMEM((2, heads, head_dim, head_dim), f32),
            pltpu.VMEM((heads, shards - 1, head_dim, head_dim), f32),
            pltpu.VMEM((3, length, head_dim), f32),
            pltpu.VMEM((heads, groups, 3, part, head_dim), bf16),
            pltpu.SMEM((2, shards - 1), f32),
            pltpu.SemaphoreType.DMA((heads,)),
            pltpu.SemaphoreType.DMA((heads,)),
            pltpu.SemaphoreType.DMA((heads,)),
            pltpu.SemaphoreType.DMA,
            pltpu.SemaphoreType.DMA((groups - 1, heads)),
            pltpu.SemaphoreType.DMA((2,)),
        ],
        compiler_params=pltpu.CompilerParams(
            collective_id=0, has_side_effects=True, vmem_limit_bytes=VMEM_BYTES - 6 * part * groups * columns
        ),
        cost_estimate=pl.CostEstimate(
            flops=heads * length * (10 * length + 10 * head_dim) * head_dim,
            bytes_accessed=7 * length * columns * 2,
            transcendentals=heads * length * (length + 4 * head_dim),
        ),
    )(doc_lengths, rates, queries, keys, values, grad_out)
    out = jax.ShapeDtypeStruct((part, groups * columns), bf16)
    return pl.pallas_call(
        write_out,
        out_shape=(out, out, out),
        in_specs=[vmem],
        out_specs=(hbm, hbm, hbm),
        scratch_shapes=[pltpu.SemaphoreType.DMA((12,))],
    )(landed)


def solution(mesh):
    return jax.shard_map(
        body,
        mesh=mesh,
        in_specs=(
            P("seq", "head"),
            P("seq", "head"),
            P("seq", "head"),
            P("seq", "head"),
            P("head"),
            P(),
        ),
        out_specs=(P(("seq", "head"), None), P(("seq", "head"), None), P(("seq", "head"), None)),
        check_vma=False,
    )
```

```python
import functools

import jax
import jax.numpy as jnp
from jax import lax
from jax.experimental import pallas as pl
from jax.experimental.pallas import tpu as pltpu
from jax.sharding import PartitionSpec as P

MESH = pl.DeviceIdType.MESH
NEVER = 1e30
VMEM_BYTES = 62 * 1024 * 1024


def dot(a, b, dims):
    return lax.dot_general(a, b, (dims, ((), ())), preferred_element_type=jnp.float32)


NN = ((1,), (0,))
NT = ((1,), (1,))
TN = ((0,), (0,))


def kernel(
    shards,
    groups,
    docs,
    lengths_hbm,
    rates_hbm,
    q_hbm,
    k_hbm,
    v_hbm,
    g_hbm,
    land,
    lengths,
    rates,
    rows_in,
    dist,
    row_dist,
    sums,
    mates,
    pair_sums,
    gathered,
    acc,
    stage,
    gaps,
    load_sem,
    mate_send,
    mate_recv,
    sum_send,
    sum_recv,
    out_send,
    out_recv,
    small_sem,
):
    heads, _, length, head_dim = rows_in.shape
    part = length // groups
    shard = lax.axis_index("seq")
    group = lax.axis_index("head")
    pairs, pair, core = shards // 2, shard // 2, lax.rem(shard, 2)
    inputs = (q_hbm, k_hbm, v_hbm, g_hbm)

    def load(h):
        columns = pl.ds(pl.multiple_of(h * head_dim, head_dim), head_dim)
        return [
            pltpu.make_async_copy(ref.at[:, columns], rows_in.at[h, i], load_sem.at[h])
            for i, ref in enumerate(inputs)
        ]

    small = [
        pltpu.make_async_copy(lengths_hbm, lengths, small_sem.at[0]),
        pltpu.make_async_copy(rates_hbm, rates, small_sem.at[1]),
    ]
    for copy in small + load(0):
        copy.start()

    barrier = pltpu.get_barrier_semaphore()
    for d in range(1, shards):
        peer = lax.rem(shard + d, shards)
        pl.semaphore_signal(barrier, inc=1, device_id=(peer, group), device_id_type=MESH)
    for d in range(1, groups):
        peer = lax.rem(group + d, groups)
        pl.semaphore_signal(barrier, inc=1, device_id=(shard, peer), device_id_type=MESH)

    first = shard * length
    for copy in small:
        copy.wait()

    def starts():
        total = jnp.int32(0)
        for i in range(docs):
            yield total
            total = total + lengths[i]

    def seg(positions):
        count = -1
        for start in starts():
            count = count + jnp.where(start <= positions, 1, 0)
        return count

    seg_first = seg(first)
    seg_last = seg(first + length - 1)
    seg_prev = seg(first - 1)
    seg_next = seg(first + length)
    wide = (length, head_dim)
    offset = lax.broadcasted_iota(jnp.int32, wide, 0)
    segment = seg(first + offset)
    where = offset.astype(jnp.float32)
    row_dist[0] = jnp.where(segment == seg_last, length - 1.0 - where, NEVER)
    row_dist[1] = jnp.where(segment == seg_first, where, NEVER)

    def summarise(h):
        pltpu.make_async_copy(rows_in.at[h], rows_in.at[h], load_sem.at[h]).wait()
        rate = rates[h]
        weighted_k = (
            rows_in[h, 1].astype(jnp.float32) * jnp.exp(-rate * row_dist[0])
        ).astype(jnp.bfloat16)
        sums[h, 0] = dot(weighted_k, rows_in[h, 2], TN)
        weighted_q = (
            rows_in[h, 0].astype(jnp.float32) * jnp.exp(-rate * row_dist[1])
        ).astype(jnp.bfloat16)
        sums[h, 1] = dot(weighted_q, rows_in[h, 3], TN)

    def swap(h):
        return pltpu.make_async_remote_copy(
            src_ref=sums.at[h],
            dst_ref=mates.at[h],
            send_sem=mate_send,
            recv_sem=mate_recv.at[h],
            device_id=(pair * 2 + 1 - core, group),
            device_id_type=MESH,
        )

    def factor(way, entry, rate):
        return jnp.exp(jnp.full((1, head_dim), -rate * gaps[way, entry]))

    def send_sums(h):
        swap(h).wait_recv()
        rate = rates[h]
        half = pl.ds(pl.multiple_of(core * (head_dim // 2), head_dim // 2), head_dim // 2)
        for way in range(2):
            pair_sums[h, way] = (
                factor(way, pairs, rate) * sums[h, way, half]
                + factor(way, pairs + 1, rate) * mates[h, way, half]
            )
        for d in range(1, pairs):
            peer = lax.rem(pair + d, pairs)
            back = (pair + d) // pairs
            for side in range(2):
                pltpu.make_async_remote_copy(
                    src_ref=pair_sums.at[h, back],
                    dst_ref=gathered.at[h, d - 1, core],
                    send_sem=sum_send,
                    recv_sem=sum_recv.at[h],
                    device_id=(peer * 2 + side, group),
                    device_id_type=MESH,
                ).start()

    lead = min(3, heads)
    summarise(0)
    pl.semaphore_wait(barrier, shards + groups - 2)
    swap(0).start()
    for h in range(1, lead):
        for copy in load(h):
            copy.start()

    for d in range(1, pairs):
        source = lax.rem(pair - d + pairs, pairs)
        ahead = (pair + pairs - d) // pairs
        same_fwd = seg((source + 1) * 2 * length - 1) == seg_prev
        same_bwd = seg(source * 2 * length) == seg_next
        gap_fwd = (2 * (d - 1) + core) * length
        gap_bwd = (2 * (pairs - d) - 1 - core) * length
        gaps[0, d - 1] = jnp.where(
            jnp.logical_and(ahead == 1, same_fwd), gap_fwd.astype(jnp.float32), NEVER
        )
        gaps[1, d - 1] = jnp.where(
            jnp.logical_and(ahead == 0, same_bwd), gap_bwd.astype(jnp.float32), NEVER
        )
    left = pair * 2 * length
    kept_fwd = seg(left + 2 * length - 1) == seg(left + length - 1)
    kept_bwd = seg(left) == seg(left + length)
    step_fwd = jnp.where(kept_fwd, float(length), NEVER)
    step_bwd = jnp.where(kept_bwd, float(length), NEVER)
    is_left = core == 0
    gaps[0, pairs - 1] = jnp.where(is_left, NEVER, 0.0)
    gaps[1, pairs - 1] = jnp.where(is_left, 0.0, NEVER)
    gaps[0, pairs] = jnp.where(is_left, step_fwd, 0.0)
    gaps[0, pairs + 1] = jnp.where(is_left, 0.0, step_fwd)
    gaps[1, pairs] = jnp.where(is_left, 0.0, step_bwd)
    gaps[1, pairs + 1] = jnp.where(is_left, step_bwd, 0.0)

    for h in range(1, lead):
        summarise(h)
        swap(h).start()
        send_sums(h - 1)

    @pl.loop(lead, heads)
    def _(h):
        for copy in load(h):
            copy.start()

    row_dist[2] = jnp.where(segment == seg_prev, where + 1.0, NEVER)
    row_dist[3] = jnp.where(segment == seg_next, length - where, NEVER)

    tile = min(256, length)
    tiles = length // tile
    across = lax.broadcasted_iota(jnp.int32, (1, length), 1)
    seg_across = seg(first + across)
    for i in range(tiles):
        down = i * tile + lax.broadcasted_iota(jnp.int32, (tile, 1), 0)
        seg_down = seg(first + down)
        gap = down - across
        dist[pl.ds(i * tile, tile), :] = jnp.where(
            jnp.logical_and(seg_down == seg_across, gap >= 0), gap.astype(jnp.float32), NEVER
        )

    order = sorted(range(1, groups), key=lambda d: abs(2 * d - groups))

    def columns_of(source, h):
        return pl.ds(pl.multiple_of((source * heads + h) * head_dim, head_dim), head_dim)

    def push(h, d):
        peer = lax.rem(group + d, groups)
        return pltpu.make_async_remote_copy(
            src_ref=stage.at[h, peer],
            dst_ref=land.at[:, :, columns_of(group, h)],
            send_sem=out_send,
            recv_sem=out_recv.at[d - 1, h],
            device_id=(shard, peer),
            device_id_type=MESH,
        )

    @pl.loop(0, heads)
    def _(h):
        @pl.when(h + lead < heads)
        def _():
            summarise(h + lead)
            swap(h + lead).start()

        @pl.when(h + lead - 1 < heads)
        def _():
            send_sums(h + lead - 1)

        rate = rates[h]
        for i in range(tiles):
            rows, seen = pl.ds(i * tile, tile), (i + 1) * tile
            q, g = rows_in[h, 0, rows], rows_in[h, 3, rows]
            k, v = rows_in[h, 1, pl.ds(0, seen)], rows_in[h, 2, pl.ds(0, seen)]
            decay = jnp.exp(-rate * dist[rows, pl.ds(0, seen)])
            p = (decay * dot(g, v, NT)).astype(jnp.bfloat16)
            a = (decay * dot(q, k, NT)).astype(jnp.bfloat16)
            acc[0, rows] = dot(p, k, NN)
            dk, dv = dot(p, q, TN), dot(a, g, TN)
            if i:
                acc[1, pl.ds(0, i * tile)] += dk[: i * tile]
                acc[2, pl.ds(0, i * tile)] += dv[: i * tile]
            acc[1, rows] = dk[i * tile :]
            acc[2, rows] = dv[i * tile :]

        pltpu.make_async_copy(gathered.at[h], gathered.at[h], sum_recv.at[h]).wait()
        state = factor(0, pairs - 1, rate) * mates[h, 0]
        back = factor(1, pairs - 1, rate) * mates[h, 1]
        for d in range(pairs - 1):
            summary = gathered[h, d].reshape(head_dim, head_dim)
            state += factor(0, d, rate) * summary
            back += factor(1, d, rate) * summary
        state = state.astype(jnp.bfloat16)
        back = back.astype(jnp.bfloat16)
        factor_in = jnp.exp(-rate * row_dist[2])
        factor_back = jnp.exp(-rate * row_dist[3])
        dq = acc[0] + dot(rows_in[h, 3], state, NT) * factor_in
        dk = acc[1] + dot(rows_in[h, 2], back, NT) * factor_back
        dv = acc[2] + dot(rows_in[h, 1], back, NN) * factor_back
        for c, total in enumerate((dq, dk, dv)):
            stage[h, :, c] = total.astype(jnp.bfloat16).reshape(groups, part, head_dim)
        for d in order:
            push(h, d).start()
        land[:, :, columns_of(group, h)] = stage[h, group]

    @pl.loop(0, heads)
    def _(h):
        for d in order:
            push(h, d).wait_recv()

    pltpu.make_async_copy(sums, sums, mate_send).wait()
    pltpu.make_async_copy(gathered, gathered, sum_send).wait()
    sent = stage.at[:, pl.ds(0, groups - 1)]
    pltpu.make_async_copy(sent, sent, out_send).wait()


def write_out(land, dq_hbm, dk_hbm, dv_hbm, write_sem):
    columns = land.shape[2]
    pieces = 4
    width = columns // pieces
    copies = []
    for c, ref in enumerate((dq_hbm, dk_hbm, dv_hbm)):
        for i in range(pieces):
            piece = pl.ds(i * width, width)
            copies.append(
                pltpu.make_async_copy(
                    land.at[c, :, piece], ref.at[:, piece], write_sem.at[c * pieces + i]
                )
            )
    for copy in copies:
        copy.start()
    for copy in copies:
        copy.wait()


def body(queries, keys, values, grad_out, rates, doc_lengths):
    length, columns = queries.shape
    heads = rates.shape[0]
    head_dim = columns // heads
    shards = lax.axis_size("seq")
    groups = lax.axis_size("head")
    part = length // groups
    docs = doc_lengths.shape[0]
    hbm = pl.BlockSpec(memory_space=pltpu.HBM)
    vmem = pl.BlockSpec(memory_space=pltpu.VMEM)
    bf16, f32 = jnp.bfloat16, jnp.float32
    landed = pl.pallas_call(
        functools.partial(kernel, shards, groups, docs),
        out_shape=pltpu.VMEM((3, part, groups * columns), bf16),
        in_specs=[hbm] * 6,
        out_specs=vmem,
        scratch_shapes=[
            pltpu.SMEM(doc_lengths.shape, jnp.int32),
            pltpu.SMEM(rates.shape, f32),
            pltpu.VMEM((heads, 4, length, head_dim), bf16),
            pltpu.VMEM((length, length), f32),
            pltpu.VMEM((4, length, head_dim), f32),
            pltpu.VMEM((heads, 2, head_dim, head_dim), f32),
            pltpu.VMEM((heads, 2, head_dim, head_dim), f32),
            pltpu.VMEM((heads, 2, head_dim // 2, head_dim), f32),
            pltpu.VMEM((heads, shards // 2 - 1, 2, head_dim // 2, head_dim), f32),
            pltpu.VMEM((3, length, head_dim), f32),
            pltpu.VMEM((heads, groups, 3, part, head_dim), bf16),
            pltpu.SMEM((2, shards // 2 + 2), f32),
            pltpu.SemaphoreType.DMA((heads,)),
            pltpu.SemaphoreType.DMA,
            pltpu.SemaphoreType.DMA((heads,)),
            pltpu.SemaphoreType.DMA,
            pltpu.SemaphoreType.DMA((heads,)),
            pltpu.SemaphoreType.DMA,
            pltpu.SemaphoreType.DMA((groups - 1, heads)),
            pltpu.SemaphoreType.DMA((2,)),
        ],
        compiler_params=pltpu.CompilerParams(
            collective_id=0, has_side_effects=True, vmem_limit_bytes=VMEM_BYTES - 6 * part * groups * columns
        ),
        cost_estimate=pl.CostEstimate(
            flops=heads * length * (10 * length + 10 * head_dim) * head_dim,
            bytes_accessed=7 * length * columns * 2,
            transcendentals=heads * length * (length + 4 * head_dim),
        ),
    )(doc_lengths, rates, queries, keys, values, grad_out)
    out = jax.ShapeDtypeStruct((part, groups * columns), bf16)
    return pl.pallas_call(
        write_out,
        out_shape=(out, out, out),
        in_specs=[pl.BlockSpec(memory_space=pl.ANY)],
        out_specs=(hbm, hbm, hbm),
        scratch_shapes=[pltpu.SemaphoreType.DMA((12,))],
        compiler_params=pltpu.CompilerParams(vmem_limit_bytes=1024 * 1024),
    )(landed)


def solution(mesh):
    return jax.shard_map(
        body,
        mesh=mesh,
        in_specs=(
            P("seq", "head"),
            P("seq", "head"),
            P("seq", "head"),
            P("seq", "head"),
            P("head"),
            P(),
        ),
        out_specs=(P(("seq", "head"), None), P(("seq", "head"), None), P(("seq", "head"), None)),
        check_vma=False,
    )
```

```python
import functools

import jax
import jax.numpy as jnp
from jax import lax
from jax.experimental import pallas as pl
from jax.experimental.pallas import tpu as pltpu
from jax.sharding import PartitionSpec as P

MESH = pl.DeviceIdType.MESH
NEVER = 1e30
VMEM_BYTES = 62 * 1024 * 1024


def dot(a, b, dims):
    return lax.dot_general(a, b, (dims, ((), ())), preferred_element_type=jnp.float32)


NN = ((1,), (0,))
NT = ((1,), (1,))
TN = ((0,), (0,))


def kernel(
    shards,
    groups,
    docs,
    lengths_hbm,
    rates_hbm,
    q_hbm,
    k_hbm,
    v_hbm,
    g_hbm,
    land,
    lengths,
    rates,
    rows_in,
    dist,
    row_dist,
    sums,
    mates,
    pair_sums,
    gathered,
    acc,
    stage,
    gaps,
    load_sem,
    mate_send,
    mate_recv,
    sum_send,
    sum_recv,
    out_send,
    out_recv,
    small_sem,
):
    heads, _, length, head_dim = rows_in.shape
    part = length // groups
    shard = lax.axis_index("seq")
    group = lax.axis_index("head")
    pairs, pair, core = shards // 2, shard // 2, lax.rem(shard, 2)
    inputs = (q_hbm, k_hbm, v_hbm, g_hbm)

    def load(h):
        columns = pl.ds(pl.multiple_of(h * head_dim, head_dim), head_dim)
        return [
            pltpu.make_async_copy(ref.at[:, columns], rows_in.at[h, i], load_sem.at[h])
            for i, ref in enumerate(inputs)
        ]

    small = [
        pltpu.make_async_copy(lengths_hbm, lengths, small_sem.at[0]),
        pltpu.make_async_copy(rates_hbm, rates, small_sem.at[1]),
    ]
    for copy in small + load(0) + load(1):
        copy.start()

    barrier = pltpu.get_barrier_semaphore()
    for d in range(1, shards):
        peer = lax.rem(shard + d, shards)
        pl.semaphore_signal(barrier, inc=1, device_id=(peer, group), device_id_type=MESH)
    for d in range(1, groups):
        peer = lax.rem(group + d, groups)
        pl.semaphore_signal(barrier, inc=1, device_id=(shard, peer), device_id_type=MESH)

    first = shard * length
    for copy in small:
        copy.wait()

    def starts():
        total = jnp.int32(0)
        for i in range(docs):
            yield total
            total = total + lengths[i]

    def seg(positions):
        count = -1
        for start in starts():
            count = count + jnp.where(start <= positions, 1, 0)
        return count

    seg_first = seg(first)
    seg_last = seg(first + length - 1)
    seg_prev = seg(first - 1)
    seg_next = seg(first + length)
    wide = (length, head_dim)
    offset = lax.broadcasted_iota(jnp.int32, wide, 0)
    segment = seg(first + offset)
    where = offset.astype(jnp.float32)
    row_dist[0] = jnp.where(segment == seg_last, length - 1.0 - where, NEVER)
    row_dist[1] = jnp.where(segment == seg_first, where, NEVER)

    def summarise(h):
        pltpu.make_async_copy(rows_in.at[h], rows_in.at[h], load_sem.at[h]).wait()
        rate = rates[h]
        weighted_k = (
            rows_in[h, 1].astype(jnp.float32) * jnp.exp(-rate * row_dist[0])
        ).astype(jnp.bfloat16)
        sums[h, 0] = dot(weighted_k, rows_in[h, 2], TN)
        weighted_q = (
            rows_in[h, 0].astype(jnp.float32) * jnp.exp(-rate * row_dist[1])
        ).astype(jnp.bfloat16)
        sums[h, 1] = dot(weighted_q, rows_in[h, 3], TN)

    def swap(h):
        return pltpu.make_async_remote_copy(
            src_ref=sums.at[h],
            dst_ref=mates.at[h],
            send_sem=mate_send,
            recv_sem=mate_recv.at[h],
            device_id=(pair * 2 + 1 - core, group),
            device_id_type=MESH,
        )

    def factor(way, entry, rate):
        return jnp.exp(jnp.full((1, head_dim), -rate * gaps[way, entry]))

    def send_sums(h):
        swap(h).wait_recv()
        rate = rates[h]
        half = pl.ds(pl.multiple_of(core * (head_dim // 2), head_dim // 2), head_dim // 2)
        for way in range(2):
            pair_sums[h, way] = (
                factor(way, pairs, rate) * sums[h, way, half]
                + factor(way, pairs + 1, rate) * mates[h, way, half]
            )
        for d in range(1, pairs):
            peer = lax.rem(pair + d, pairs)
            back = (pair + d) // pairs
            for side in range(2):
                pltpu.make_async_remote_copy(
                    src_ref=pair_sums.at[h, back],
                    dst_ref=gathered.at[h, d - 1, core],
                    send_sem=sum_send,
                    recv_sem=sum_recv.at[h],
                    device_id=(peer * 2 + side, group),
                    device_id_type=MESH,
                ).start()

    summarise(0)

    row_dist[2] = jnp.where(segment == seg_prev, where + 1.0, NEVER)
    row_dist[3] = jnp.where(segment == seg_next, length - where, NEVER)

    tile = min(256, length)
    tiles = length // tile
    across = lax.broadcasted_iota(jnp.int32, (1, length), 1)
    seg_across = seg(first + across)
    for i in range(tiles):
        down = i * tile + lax.broadcasted_iota(jnp.int32, (tile, 1), 0)
        seg_down = seg(first + down)
        gap = down - across
        dist[pl.ds(i * tile, tile), :] = jnp.where(
            jnp.logical_and(seg_down == seg_across, gap >= 0), gap.astype(jnp.float32), NEVER
        )

    for d in range(1, pairs):
        source = lax.rem(pair - d + pairs, pairs)
        ahead = (pair + pairs - d) // pairs
        same_fwd = seg((source + 1) * 2 * length - 1) == seg_prev
        same_bwd = seg(source * 2 * length) == seg_next
        gap_fwd = (2 * (d - 1) + core) * length
        gap_bwd = (2 * (pairs - d) - 1 - core) * length
        gaps[0, d - 1] = jnp.where(
            jnp.logical_and(ahead == 1, same_fwd), gap_fwd.astype(jnp.float32), NEVER
        )
        gaps[1, d - 1] = jnp.where(
            jnp.logical_and(ahead == 0, same_bwd), gap_bwd.astype(jnp.float32), NEVER
        )
    left = pair * 2 * length
    kept_fwd = seg(left + 2 * length - 1) == seg(left + length - 1)
    kept_bwd = seg(left) == seg(left + length)
    step_fwd = jnp.where(kept_fwd, float(length), NEVER)
    step_bwd = jnp.where(kept_bwd, float(length), NEVER)
    is_left = core == 0
    gaps[0, pairs - 1] = jnp.where(is_left, NEVER, 0.0)
    gaps[1, pairs - 1] = jnp.where(is_left, 0.0, NEVER)
    gaps[0, pairs] = jnp.where(is_left, step_fwd, 0.0)
    gaps[0, pairs + 1] = jnp.where(is_left, 0.0, step_fwd)
    gaps[1, pairs] = jnp.where(is_left, 0.0, step_bwd)
    gaps[1, pairs + 1] = jnp.where(is_left, step_bwd, 0.0)

    pl.semaphore_wait(barrier, shards + groups - 2)
    swap(0).start()
    summarise(1)
    swap(1).start()
    send_sums(0)

    order = sorted(range(1, groups), key=lambda d: abs(2 * d - groups))

    def columns_of(source, h):
        return pl.ds(pl.multiple_of((source * heads + h) * head_dim, head_dim), head_dim)

    def push(h, d):
        peer = lax.rem(group + d, groups)
        return pltpu.make_async_remote_copy(
            src_ref=stage.at[h, peer],
            dst_ref=land.at[:, :, columns_of(group, h)],
            send_sem=out_send,
            recv_sem=out_recv.at[d - 1, h],
            device_id=(shard, peer),
            device_id_type=MESH,
        )

    @pl.loop(0, heads)
    def _(h):
        @pl.when(h + 2 < heads)
        def _():
            for copy in load(h + 2):
                copy.start()

        rate = rates[h]
        for i in range(tiles):
            rows, seen = pl.ds(i * tile, tile), (i + 1) * tile
            q, g = rows_in[h, 0, rows], rows_in[h, 3, rows]
            k, v = rows_in[h, 1, pl.ds(0, seen)], rows_in[h, 2, pl.ds(0, seen)]
            decay = jnp.exp(-rate * dist[rows, pl.ds(0, seen)])
            p = (decay * dot(g, v, NT)).astype(jnp.bfloat16)
            a = (decay * dot(q, k, NT)).astype(jnp.bfloat16)
            acc[0, rows] = dot(p, k, NN)
            dk, dv = dot(p, q, TN), dot(a, g, TN)
            if i:
                acc[1, pl.ds(0, i * tile)] += dk[: i * tile]
                acc[2, pl.ds(0, i * tile)] += dv[: i * tile]
            acc[1, rows] = dk[i * tile :]
            acc[2, rows] = dv[i * tile :]

        @pl.when(h + 1 < heads)
        def _():
            send_sums(h + 1)

        @pl.when(h + 2 < heads)
        def _():
            summarise(h + 2)
            swap(h + 2).start()

        pltpu.make_async_copy(gathered.at[h], gathered.at[h], sum_recv.at[h]).wait()
        state = factor(0, pairs - 1, rate) * mates[h, 0]
        back = factor(1, pairs - 1, rate) * mates[h, 1]
        for d in range(pairs - 1):
            summary = gathered[h, d].reshape(head_dim, head_dim)
            state += factor(0, d, rate) * summary
            back += factor(1, d, rate) * summary
        state = state.astype(jnp.bfloat16)
        back = back.astype(jnp.bfloat16)
        factor_in = jnp.exp(-rate * row_dist[2])
        factor_back = jnp.exp(-rate * row_dist[3])
        dq = acc[0] + dot(rows_in[h, 3], state, NT) * factor_in
        dk = acc[1] + dot(rows_in[h, 2], back, NT) * factor_back
        dv = acc[2] + dot(rows_in[h, 1], back, NN) * factor_back
        for c, total in enumerate((dq, dk, dv)):
            stage[h, :, c] = total.astype(jnp.bfloat16).reshape(groups, part, head_dim)
        for d in order:
            push(h, d).start()
        land[:, :, columns_of(group, h)] = stage[h, group]

    @pl.loop(0, heads)
    def _(h):
        for d in order:
            push(h, d).wait_recv()

    pltpu.make_async_copy(sums, sums, mate_send).wait()
    pltpu.make_async_copy(gathered, gathered, sum_send).wait()
    sent = stage.at[:, pl.ds(0, groups - 1)]
    pltpu.make_async_copy(sent, sent, out_send).wait()


def write_out(land, dq_hbm, dk_hbm, dv_hbm, write_sem):
    columns = land.shape[2]
    pieces = 4
    width = columns // pieces
    copies = []
    for c, ref in enumerate((dq_hbm, dk_hbm, dv_hbm)):
        for i in range(pieces):
            piece = pl.ds(i * width, width)
            copies.append(
                pltpu.make_async_copy(
                    land.at[c, :, piece], ref.at[:, piece], write_sem.at[c * pieces + i]
                )
            )
    for copy in copies:
        copy.start()
    for copy in copies:
        copy.wait()


def body(queries, keys, values, grad_out, rates, doc_lengths):
    length, columns = queries.shape
    heads = rates.shape[0]
    head_dim = columns // heads
    shards = lax.axis_size("seq")
    groups = lax.axis_size("head")
    part = length // groups
    docs = doc_lengths.shape[0]
    hbm = pl.BlockSpec(memory_space=pltpu.HBM)
    vmem = pl.BlockSpec(memory_space=pltpu.VMEM)
    bf16, f32 = jnp.bfloat16, jnp.float32
    landed = pl.pallas_call(
        functools.partial(kernel, shards, groups, docs),
        out_shape=pltpu.VMEM((3, part, groups * columns), bf16),
        in_specs=[hbm] * 6,
        out_specs=vmem,
        scratch_shapes=[
            pltpu.SMEM(doc_lengths.shape, jnp.int32),
            pltpu.SMEM(rates.shape, f32),
            pltpu.VMEM((heads, 4, length, head_dim), bf16),
            pltpu.VMEM((length, length), f32),
            pltpu.VMEM((4, length, head_dim), f32),
            pltpu.VMEM((heads, 2, head_dim, head_dim), f32),
            pltpu.VMEM((heads, 2, head_dim, head_dim), f32),
            pltpu.VMEM((heads, 2, head_dim // 2, head_dim), f32),
            pltpu.VMEM((heads, shards // 2 - 1, 2, head_dim // 2, head_dim), f32),
            pltpu.VMEM((3, length, head_dim), f32),
            pltpu.VMEM((heads, groups, 3, part, head_dim), bf16),
            pltpu.SMEM((2, shards // 2 + 2), f32),
            pltpu.SemaphoreType.DMA((heads,)),
            pltpu.SemaphoreType.DMA,
            pltpu.SemaphoreType.DMA((heads,)),
            pltpu.SemaphoreType.DMA,
            pltpu.SemaphoreType.DMA((heads,)),
            pltpu.SemaphoreType.DMA,
            pltpu.SemaphoreType.DMA((groups - 1, heads)),
            pltpu.SemaphoreType.DMA((2,)),
        ],
        compiler_params=pltpu.CompilerParams(
            collective_id=0, has_side_effects=True, vmem_limit_bytes=VMEM_BYTES - 6 * part * groups * columns
        ),
        cost_estimate=pl.CostEstimate(
            flops=heads * length * (10 * length + 10 * head_dim) * head_dim,
            bytes_accessed=7 * length * columns * 2,
            transcendentals=heads * length * (length + 4 * head_dim),
        ),
    )(doc_lengths, rates, queries, keys, values, grad_out)
    out = jax.ShapeDtypeStruct((part, groups * columns), bf16)
    return pl.pallas_call(
        write_out,
        out_shape=(out, out, out),
        in_specs=[pl.BlockSpec(memory_space=pl.ANY)],
        out_specs=(hbm, hbm, hbm),
        scratch_shapes=[pltpu.SemaphoreType.DMA((12,))],
        compiler_params=pltpu.CompilerParams(vmem_limit_bytes=1024 * 1024),
    )(landed)


def solution(mesh):
    return jax.shard_map(
        body,
        mesh=mesh,
        in_specs=(
            P("seq", "head"),
            P("seq", "head"),
            P("seq", "head"),
            P("seq", "head"),
            P("head"),
            P(),
        ),
        out_specs=(P(("seq", "head"), None), P(("seq", "head"), None), P(("seq", "head"), None)),
        check_vma=False,
    )
```

```python
import functools

import jax
import jax.numpy as jnp
from jax import lax
from jax.experimental import pallas as pl
from jax.experimental.pallas import tpu as pltpu
from jax.sharding import PartitionSpec as P

MESH = pl.DeviceIdType.MESH
NEVER = 1e30
VMEM_BYTES = 62 * 1024 * 1024


def dot(a, b, dims):
    return lax.dot_general(a, b, (dims, ((), ())), preferred_element_type=jnp.float32)


NN = ((1,), (0,))
NT = ((1,), (1,))
TN = ((0,), (0,))


def kernel(
    shards,
    groups,
    docs,
    lengths_hbm,
    rates_hbm,
    q_hbm,
    k_hbm,
    v_hbm,
    g_hbm,
    land,
    lengths,
    rates,
    rows_in,
    dist,
    dist_t,
    row_dist,
    sums,
    mates,
    pair_sums,
    gathered,
    acc,
    stage,
    gaps,
    load_sem,
    mate_send,
    mate_recv,
    sum_send,
    sum_recv,
    out_send,
    out_recv,
    small_sem,
):
    heads, _, length, head_dim = rows_in.shape
    part = length // groups
    shard = lax.axis_index("seq")
    group = lax.axis_index("head")
    pairs, pair, core = shards // 2, shard // 2, lax.rem(shard, 2)
    inputs = (q_hbm, k_hbm, v_hbm, g_hbm)

    def load(h):
        columns = pl.ds(pl.multiple_of(h * head_dim, head_dim), head_dim)
        return [
            pltpu.make_async_copy(ref.at[:, columns], rows_in.at[h, i], load_sem.at[h])
            for i, ref in enumerate(inputs)
        ]

    small = [
        pltpu.make_async_copy(lengths_hbm, lengths, small_sem.at[0]),
        pltpu.make_async_copy(rates_hbm, rates, small_sem.at[1]),
    ]
    for copy in small + load(0) + load(1):
        copy.start()

    barrier = pltpu.get_barrier_semaphore()
    for d in range(1, shards):
        peer = lax.rem(shard + d, shards)
        pl.semaphore_signal(barrier, inc=1, device_id=(peer, group), device_id_type=MESH)
    for d in range(1, groups):
        peer = lax.rem(group + d, groups)
        pl.semaphore_signal(barrier, inc=1, device_id=(shard, peer), device_id_type=MESH)

    first = shard * length
    for copy in small:
        copy.wait()

    def starts():
        total = jnp.int32(0)
        for i in range(docs):
            yield total
            total = total + lengths[i]

    def seg(positions):
        count = -1
        for start in starts():
            count = count + jnp.where(start <= positions, 1, 0)
        return count

    seg_first = seg(first)
    seg_last = seg(first + length - 1)
    seg_prev = seg(first - 1)
    seg_next = seg(first + length)
    wide = (length, head_dim)
    offset = lax.broadcasted_iota(jnp.int32, wide, 0)
    segment = seg(first + offset)
    where = offset.astype(jnp.float32)
    row_dist[0] = jnp.where(segment == seg_last, length - 1.0 - where, NEVER)
    row_dist[1] = jnp.where(segment == seg_first, where, NEVER)

    def summarise(h):
        pltpu.make_async_copy(rows_in.at[h], rows_in.at[h], load_sem.at[h]).wait()
        rate = rates[h]
        weighted_k = (
            rows_in[h, 1].astype(jnp.float32) * jnp.exp(-rate * row_dist[0])
        ).astype(jnp.bfloat16)
        sums[h, 0] = dot(weighted_k, rows_in[h, 2], TN)
        weighted_q = (
            rows_in[h, 0].astype(jnp.float32) * jnp.exp(-rate * row_dist[1])
        ).astype(jnp.bfloat16)
        sums[h, 1] = dot(weighted_q, rows_in[h, 3], TN)

    def swap(h):
        return pltpu.make_async_remote_copy(
            src_ref=sums.at[h],
            dst_ref=mates.at[h],
            send_sem=mate_send,
            recv_sem=mate_recv.at[h],
            device_id=(pair * 2 + 1 - core, group),
            device_id_type=MESH,
        )

    def factor(way, entry, rate):
        return jnp.exp(jnp.full((1, head_dim), -rate * gaps[way, entry]))

    def send_sums(h):
        swap(h).wait_recv()
        rate = rates[h]
        half = pl.ds(pl.multiple_of(core * (head_dim // 2), head_dim // 2), head_dim // 2)
        for way in range(2):
            pair_sums[h, way] = (
                factor(way, pairs, rate) * sums[h, way, half]
                + factor(way, pairs + 1, rate) * mates[h, way, half]
            )
        for d in range(1, pairs):
            peer = lax.rem(pair + d, pairs)
            back = (pair + d) // pairs
            for side in range(2):
                pltpu.make_async_remote_copy(
                    src_ref=pair_sums.at[h, back],
                    dst_ref=gathered.at[h, d - 1, core],
                    send_sem=sum_send,
                    recv_sem=sum_recv.at[h],
                    device_id=(peer * 2 + side, group),
                    device_id_type=MESH,
                ).start()

    summarise(0)

    row_dist[2] = jnp.where(segment == seg_prev, where + 1.0, NEVER)
    row_dist[3] = jnp.where(segment == seg_next, length - where, NEVER)

    tile = min(256, length)
    tiles = length // tile
    across = lax.broadcasted_iota(jnp.int32, (1, length), 1)
    seg_across = seg(first + across)
    for i in range(tiles):
        down = i * tile + lax.broadcasted_iota(jnp.int32, (tile, 1), 0)
        seg_down = seg(first + down)
        gap = down - across
        dist[pl.ds(i * tile, tile), :] = jnp.where(
            jnp.logical_and(seg_down == seg_across, gap >= 0), gap.astype(jnp.float32), NEVER
        )
        dist_t[pl.ds(i * tile, tile), :] = jnp.where(
            jnp.logical_and(seg_down == seg_across, gap <= 0), -gap.astype(jnp.float32), NEVER
        )

    for d in range(1, pairs):
        source = lax.rem(pair - d + pairs, pairs)
        ahead = (pair + pairs - d) // pairs
        same_fwd = seg((source + 1) * 2 * length - 1) == seg_prev
        same_bwd = seg(source * 2 * length) == seg_next
        gap_fwd = (2 * (d - 1) + core) * length
        gap_bwd = (2 * (pairs - d) - 1 - core) * length
        gaps[0, d - 1] = jnp.where(
            jnp.logical_and(ahead == 1, same_fwd), gap_fwd.astype(jnp.float32), NEVER
        )
        gaps[1, d - 1] = jnp.where(
            jnp.logical_and(ahead == 0, same_bwd), gap_bwd.astype(jnp.float32), NEVER
        )
    left = pair * 2 * length
    kept_fwd = seg(left + 2 * length - 1) == seg(left + length - 1)
    kept_bwd = seg(left) == seg(left + length)
    step_fwd = jnp.where(kept_fwd, float(length), NEVER)
    step_bwd = jnp.where(kept_bwd, float(length), NEVER)
    is_left = core == 0
    gaps[0, pairs - 1] = jnp.where(is_left, NEVER, 0.0)
    gaps[1, pairs - 1] = jnp.where(is_left, 0.0, NEVER)
    gaps[0, pairs] = jnp.where(is_left, step_fwd, 0.0)
    gaps[0, pairs + 1] = jnp.where(is_left, 0.0, step_fwd)
    gaps[1, pairs] = jnp.where(is_left, 0.0, step_bwd)
    gaps[1, pairs + 1] = jnp.where(is_left, step_bwd, 0.0)

    pl.semaphore_wait(barrier, shards + groups - 2)
    swap(0).start()
    summarise(1)
    swap(1).start()
    send_sums(0)

    order = sorted(range(1, groups), key=lambda d: abs(2 * d - groups))

    def crosses(d):
        peer = lax.rem(group + d, groups)
        return (2 * group < groups) != (2 * peer < groups)

    def columns_of(source, h):
        return pl.ds(pl.multiple_of((source * heads + h) * head_dim, head_dim), head_dim)

    def push(h, d):
        peer = lax.rem(group + d, groups)
        return pltpu.make_async_remote_copy(
            src_ref=stage.at[h, peer],
            dst_ref=land.at[:, :, columns_of(group, h)],
            send_sem=out_send,
            recv_sem=out_recv.at[d - 1, h],
            device_id=(shard, peer),
            device_id_type=MESH,
        )

    @pl.loop(0, heads)
    def _(h):
        @pl.when(h + 2 < heads)
        def _():
            for copy in load(h + 2):
                copy.start()

        rate = rates[h]
        for i in range(tiles):
            rows = pl.ds(i * tile, tile)
            seen = pl.ds(0, (i + 1) * tile)
            later = pl.ds(i * tile, length - i * tile)
            decay = jnp.exp(-rate * dist[rows, seen])
            p = decay * dot(rows_in[h, 3, rows], rows_in[h, 2, seen], NT)
            acc[0, rows] = dot(p.astype(jnp.bfloat16), rows_in[h, 1, seen], NN)
            decay_t = jnp.exp(-rate * dist_t[rows, later])
            p_t = decay_t * dot(rows_in[h, 2, rows], rows_in[h, 3, later], NT)
            acc[1, rows] = dot(p_t.astype(jnp.bfloat16), rows_in[h, 0, later], NN)
            a_t = decay_t * dot(rows_in[h, 1, rows], rows_in[h, 0, later], NT)
            acc[2, rows] = dot(a_t.astype(jnp.bfloat16), rows_in[h, 3, later], NN)

        @pl.when(h + 1 < heads)
        def _():
            send_sums(h + 1)

        @pl.when(h + 2 < heads)
        def _():
            summarise(h + 2)
            swap(h + 2).start()

        pltpu.make_async_copy(gathered.at[h], gathered.at[h], sum_recv.at[h]).wait()
        state = factor(0, pairs - 1, rate) * mates[h, 0]
        back = factor(1, pairs - 1, rate) * mates[h, 1]
        for d in range(pairs - 1):
            summary = gathered[h, d].reshape(head_dim, head_dim)
            state += factor(0, d, rate) * summary
            back += factor(1, d, rate) * summary
        state = state.astype(jnp.bfloat16)
        back = back.astype(jnp.bfloat16)
        factor_in = jnp.exp(-rate * row_dist[2])
        factor_back = jnp.exp(-rate * row_dist[3])
        dq = acc[0] + dot(rows_in[h, 3], state, NT) * factor_in
        dk = acc[1] + dot(rows_in[h, 2], back, NT) * factor_back
        dv = acc[2] + dot(rows_in[h, 1], back, NN) * factor_back
        for c, total in enumerate((dq, dk, dv)):
            stage[h, :, c] = total.astype(jnp.bfloat16).reshape(groups, part, head_dim)
        for far in (True, False):
            for d in order:

                @pl.when(crosses(d) == far)
                def _():
                    push(h, d).start()

        land[:, :, columns_of(group, h)] = stage[h, group]

    @pl.loop(0, heads)
    def _(h):
        for d in order:
            push(h, d).wait_recv()

    pltpu.make_async_copy(sums, sums, mate_send).wait()
    pltpu.make_async_copy(gathered, gathered, sum_send).wait()
    sent = stage.at[:, pl.ds(0, groups - 1)]
    pltpu.make_async_copy(sent, sent, out_send).wait()


def write_out(land, dq_hbm, dk_hbm, dv_hbm, write_sem):
    columns = land.shape[2]
    pieces = 4
    width = columns // pieces
    copies = []
    for c, ref in enumerate((dq_hbm, dk_hbm, dv_hbm)):
        for i in range(pieces):
            piece = pl.ds(i * width, width)
            copies.append(
                pltpu.make_async_copy(
                    land.at[c, :, piece], ref.at[:, piece], write_sem.at[c * pieces + i]
                )
            )
    for copy in copies:
        copy.start()
    for copy in copies:
        copy.wait()


def body(queries, keys, values, grad_out, rates, doc_lengths):
    length, columns = queries.shape
    heads = rates.shape[0]
    head_dim = columns // heads
    shards = lax.axis_size("seq")
    groups = lax.axis_size("head")
    part = length // groups
    docs = doc_lengths.shape[0]
    hbm = pl.BlockSpec(memory_space=pltpu.HBM)
    vmem = pl.BlockSpec(memory_space=pltpu.VMEM)
    bf16, f32 = jnp.bfloat16, jnp.float32
    landed = pl.pallas_call(
        functools.partial(kernel, shards, groups, docs),
        out_shape=pltpu.VMEM((3, part, groups * columns), bf16),
        in_specs=[hbm] * 6,
        out_specs=vmem,
        scratch_shapes=[
            pltpu.SMEM(doc_lengths.shape, jnp.int32),
            pltpu.SMEM(rates.shape, f32),
            pltpu.VMEM((heads, 4, length, head_dim), bf16),
            pltpu.VMEM((length, length), f32),
            pltpu.VMEM((length, length), f32),
            pltpu.VMEM((4, length, head_dim), f32),
            pltpu.VMEM((heads, 2, head_dim, head_dim), f32),
            pltpu.VMEM((heads, 2, head_dim, head_dim), f32),
            pltpu.VMEM((heads, 2, head_dim // 2, head_dim), f32),
            pltpu.VMEM((heads, shards // 2 - 1, 2, head_dim // 2, head_dim), f32),
            pltpu.VMEM((3, length, head_dim), f32),
            pltpu.VMEM((heads, groups, 3, part, head_dim), bf16),
            pltpu.SMEM((2, shards // 2 + 2), f32),
            pltpu.SemaphoreType.DMA((heads,)),
            pltpu.SemaphoreType.DMA,
            pltpu.SemaphoreType.DMA((heads,)),
            pltpu.SemaphoreType.DMA,
            pltpu.SemaphoreType.DMA((heads,)),
            pltpu.SemaphoreType.DMA,
            pltpu.SemaphoreType.DMA((groups - 1, heads)),
            pltpu.SemaphoreType.DMA((2,)),
        ],
        compiler_params=pltpu.CompilerParams(
            collective_id=0, has_side_effects=True, vmem_limit_bytes=VMEM_BYTES - 6 * part * groups * columns
        ),
        cost_estimate=pl.CostEstimate(
            flops=heads * length * (10 * length + 10 * head_dim) * head_dim,
            bytes_accessed=7 * length * columns * 2,
            transcendentals=heads * length * (length + 4 * head_dim),
        ),
    )(doc_lengths, rates, queries, keys, values, grad_out)
    out = jax.ShapeDtypeStruct((part, groups * columns), bf16)
    return pl.pallas_call(
        write_out,
        out_shape=(out, out, out),
        in_specs=[pl.BlockSpec(memory_space=pl.ANY)],
        out_specs=(hbm, hbm, hbm),
        scratch_shapes=[pltpu.SemaphoreType.DMA((12,))],
        compiler_params=pltpu.CompilerParams(vmem_limit_bytes=1024 * 1024),
    )(landed)


def solution(mesh):
    return jax.shard_map(
        body,
        mesh=mesh,
        in_specs=(
            P("seq", "head"),
            P("seq", "head"),
            P("seq", "head"),
            P("seq", "head"),
            P("head"),
            P(),
        ),
        out_specs=(P(("seq", "head"), None), P(("seq", "head"), None), P(("seq", "head"), None)),
        check_vma=False,
    )
```

```python
import functools

import jax
import jax.numpy as jnp
from jax import lax
from jax.experimental import pallas as pl
from jax.experimental.pallas import tpu as pltpu
from jax.sharding import PartitionSpec as P

MESH = pl.DeviceIdType.MESH
NEVER = 1e30
VMEM_BYTES = 62 * 1024 * 1024


def dot(a, b, dims):
    return lax.dot_general(a, b, (dims, ((), ())), preferred_element_type=jnp.float32)


NN = ((1,), (0,))
NT = ((1,), (1,))
TN = ((0,), (0,))


def kernel(
    shards,
    groups,
    docs,
    lengths_hbm,
    rates_hbm,
    q_hbm,
    k_hbm,
    v_hbm,
    g_hbm,
    land,
    lengths,
    rates,
    rows_in,
    dist,
    dist_t,
    row_dist,
    sums,
    mates,
    pair_sums,
    gathered,
    acc,
    stage,
    gaps,
    load_sem,
    mate_send,
    mate_recv,
    sum_send,
    sum_recv,
    out_send,
    out_recv,
    small_sem,
):
    heads, _, length, head_dim = rows_in.shape
    part = length // groups
    shard = lax.axis_index("seq")
    group = lax.axis_index("head")
    pairs, pair, core = shards // 2, shard // 2, lax.rem(shard, 2)
    inputs = (q_hbm, k_hbm, v_hbm, g_hbm)

    def load(h):
        columns = pl.ds(pl.multiple_of(h * head_dim, head_dim), head_dim)
        return [
            pltpu.make_async_copy(ref.at[:, columns], rows_in.at[h, i], load_sem.at[h])
            for i, ref in enumerate(inputs)
        ]

    small = [
        pltpu.make_async_copy(lengths_hbm, lengths, small_sem.at[0]),
        pltpu.make_async_copy(rates_hbm, rates, small_sem.at[1]),
    ]
    for copy in small + load(0) + load(1):
        copy.start()

    barrier = pltpu.get_barrier_semaphore()
    for d in range(1, shards):
        peer = lax.rem(shard + d, shards)
        pl.semaphore_signal(barrier, inc=1, device_id=(peer, group), device_id_type=MESH)
    for d in range(1, groups):
        peer = lax.rem(group + d, groups)
        pl.semaphore_signal(barrier, inc=1, device_id=(shard, peer), device_id_type=MESH)

    first = shard * length
    for copy in small:
        copy.wait()

    def starts():
        total = jnp.int32(0)
        for i in range(docs):
            yield total
            total = total + lengths[i]

    def seg(positions):
        count = -1
        for start in starts():
            count = count + jnp.where(start <= positions, 1, 0)
        return count

    seg_first = seg(first)
    seg_last = seg(first + length - 1)
    seg_prev = seg(first - 1)
    seg_next = seg(first + length)
    wide = (length, head_dim)
    offset = lax.broadcasted_iota(jnp.int32, wide, 0)
    segment = seg(first + offset)
    where = offset.astype(jnp.float32)
    row_dist[0] = jnp.where(segment == seg_last, length - 1.0 - where, NEVER)
    row_dist[1] = jnp.where(segment == seg_first, where, NEVER)

    def summarise(h):
        pltpu.make_async_copy(rows_in.at[h], rows_in.at[h], load_sem.at[h]).wait()
        rate = rates[h]
        weighted_k = (
            rows_in[h, 1].astype(jnp.float32) * jnp.exp(-rate * row_dist[0])
        ).astype(jnp.bfloat16)
        sums[h, 0] = dot(weighted_k, rows_in[h, 2], TN)
        weighted_q = (
            rows_in[h, 0].astype(jnp.float32) * jnp.exp(-rate * row_dist[1])
        ).astype(jnp.bfloat16)
        sums[h, 1] = dot(weighted_q, rows_in[h, 3], TN)

    def swap(h):
        return pltpu.make_async_remote_copy(
            src_ref=sums.at[h],
            dst_ref=mates.at[h],
            send_sem=mate_send,
            recv_sem=mate_recv.at[h],
            device_id=(pair * 2 + 1 - core, group),
            device_id_type=MESH,
        )

    def factor(way, entry, rate):
        return jnp.exp(jnp.full((1, head_dim), -rate * gaps[way, entry]))

    def send_sums(h):
        swap(h).wait_recv()
        rate = rates[h]
        half = pl.ds(pl.multiple_of(core * (head_dim // 2), head_dim // 2), head_dim // 2)
        for way in range(2):
            pair_sums[h, way] = (
                factor(way, pairs, rate) * sums[h, way, half]
                + factor(way, pairs + 1, rate) * mates[h, way, half]
            )
        for d in range(1, pairs):
            peer = lax.rem(pair + d, pairs)
            back = (pair + d) // pairs
            for side in range(2):
                pltpu.make_async_remote_copy(
                    src_ref=pair_sums.at[h, back],
                    dst_ref=gathered.at[h, d - 1, core],
                    send_sem=sum_send,
                    recv_sem=sum_recv.at[h],
                    device_id=(peer * 2 + side, group),
                    device_id_type=MESH,
                ).start()

    summarise(0)

    row_dist[2] = jnp.where(segment == seg_prev, where + 1.0, NEVER)
    row_dist[3] = jnp.where(segment == seg_next, length - where, NEVER)

    tile = min(256, length)
    tiles = length // tile
    across = lax.broadcasted_iota(jnp.int32, (1, length), 1)
    seg_across = seg(first + across)
    for i in range(tiles):
        down = i * tile + lax.broadcasted_iota(jnp.int32, (tile, 1), 0)
        seg_down = seg(first + down)
        gap = down - across
        dist[pl.ds(i * tile, tile), :] = jnp.where(
            jnp.logical_and(seg_down == seg_across, gap >= 0), gap.astype(jnp.float32), NEVER
        )
        dist_t[pl.ds(i * tile, tile), :] = jnp.where(
            jnp.logical_and(seg_down == seg_across, gap <= 0), -gap.astype(jnp.float32), NEVER
        )

    for d in range(1, pairs):
        source = lax.rem(pair - d + pairs, pairs)
        ahead = (pair + pairs - d) // pairs
        same_fwd = seg((source + 1) * 2 * length - 1) == seg_prev
        same_bwd = seg(source * 2 * length) == seg_next
        gap_fwd = (2 * (d - 1) + core) * length
        gap_bwd = (2 * (pairs - d) - 1 - core) * length
        gaps[0, d - 1] = jnp.where(
            jnp.logical_and(ahead == 1, same_fwd), gap_fwd.astype(jnp.float32), NEVER
        )
        gaps[1, d - 1] = jnp.where(
            jnp.logical_and(ahead == 0, same_bwd), gap_bwd.astype(jnp.float32), NEVER
        )
    left = pair * 2 * length
    kept_fwd = seg(left + 2 * length - 1) == seg(left + length - 1)
    kept_bwd = seg(left) == seg(left + length)
    step_fwd = jnp.where(kept_fwd, float(length), NEVER)
    step_bwd = jnp.where(kept_bwd, float(length), NEVER)
    is_left = core == 0
    gaps[0, pairs - 1] = jnp.where(is_left, NEVER, 0.0)
    gaps[1, pairs - 1] = jnp.where(is_left, 0.0, NEVER)
    gaps[0, pairs] = jnp.where(is_left, step_fwd, 0.0)
    gaps[0, pairs + 1] = jnp.where(is_left, 0.0, step_fwd)
    gaps[1, pairs] = jnp.where(is_left, 0.0, step_bwd)
    gaps[1, pairs + 1] = jnp.where(is_left, step_bwd, 0.0)

    pl.semaphore_wait(barrier, shards + groups - 2)
    swap(0).start()
    summarise(1)
    swap(1).start()
    send_sums(0)

    order = sorted(range(1, groups), key=lambda d: abs(2 * d - groups))

    def crosses(d):
        peer = lax.rem(group + d, groups)
        return (2 * group < groups) != (2 * peer < groups)

    def columns_of(source, h):
        return pl.ds(pl.multiple_of((source * heads + h) * head_dim, head_dim), head_dim)

    def push(h, d):
        peer = lax.rem(group + d, groups)
        return pltpu.make_async_remote_copy(
            src_ref=stage.at[h, peer],
            dst_ref=land.at[:, :, columns_of(group, h)],
            send_sem=out_send,
            recv_sem=out_recv.at[d - 1, h],
            device_id=(shard, peer),
            device_id_type=MESH,
        )

    def push_across(h):
        for d in order:

            @pl.when(crosses(d))
            def _():
                push(h, d).start()

    inner = jnp.logical_and(group > 0, group < groups - 1)
    end = jnp.where(2 * group < groups, 0, groups - 1)
    from_end = lax.rem(group - end + groups, groups)

    @pl.loop(0, heads)
    def _(h):
        @pl.when(h + 2 < heads)
        def _():
            for copy in load(h + 2):
                copy.start()

        rate = rates[h]
        for i in range(tiles):
            rows = pl.ds(i * tile, tile)
            seen = pl.ds(0, (i + 1) * tile)
            later = pl.ds(i * tile, length - i * tile)
            decay = jnp.exp(-rate * dist[rows, seen])
            p = decay * dot(rows_in[h, 3, rows], rows_in[h, 2, seen], NT)
            acc[0, rows] = dot(p.astype(jnp.bfloat16), rows_in[h, 1, seen], NN)
            decay_t = jnp.exp(-rate * dist_t[rows, later])
            p_t = decay_t * dot(rows_in[h, 2, rows], rows_in[h, 3, later], NT)
            acc[1, rows] = dot(p_t.astype(jnp.bfloat16), rows_in[h, 0, later], NN)
            a_t = decay_t * dot(rows_in[h, 1, rows], rows_in[h, 0, later], NT)
            acc[2, rows] = dot(a_t.astype(jnp.bfloat16), rows_in[h, 3, later], NN)

        @pl.when(h + 1 < heads)
        def _():
            send_sums(h + 1)

        @pl.when(h + 2 < heads)
        def _():
            summarise(h + 2)
            swap(h + 2).start()

        pltpu.make_async_copy(gathered.at[h], gathered.at[h], sum_recv.at[h]).wait()
        state = factor(0, pairs - 1, rate) * mates[h, 0]
        back = factor(1, pairs - 1, rate) * mates[h, 1]
        for d in range(pairs - 1):
            summary = gathered[h, d].reshape(head_dim, head_dim)
            state += factor(0, d, rate) * summary
            back += factor(1, d, rate) * summary
        state = state.astype(jnp.bfloat16)
        back = back.astype(jnp.bfloat16)
        factor_in = jnp.exp(-rate * row_dist[2])
        factor_back = jnp.exp(-rate * row_dist[3])
        dq = acc[0] + dot(rows_in[h, 3], state, NT) * factor_in
        dk = acc[1] + dot(rows_in[h, 2], back, NT) * factor_back
        dv = acc[2] + dot(rows_in[h, 1], back, NN) * factor_back
        for c, total in enumerate((dq, dk, dv)):
            stage[h, :, c] = total.astype(jnp.bfloat16).reshape(groups, part, head_dim)
        @pl.when(jnp.logical_not(inner))
        def _():
            push_across(h)

        @pl.when(jnp.logical_and(inner, lax.rem(h, 4) == 0))
        def _():
            push_across(h // 4)

        for d in order:

            @pl.when(jnp.logical_not(crosses(d)))
            def _():
                push(h, d).start()

        land[:, :, columns_of(group, h)] = stage[h, group]

    pushed = (heads + 3) // 4

    @pl.when(inner)
    def _():
        @pl.loop(pushed, heads)
        def _(h):
            push(h - 1, from_end).wait_recv()
            push_across(h)

    @pl.loop(0, heads)
    def _(h):
        paced = jnp.logical_and(inner, jnp.logical_and(h >= pushed - 1, h < heads - 1))
        for d in order:

            @pl.when(jnp.logical_not(jnp.logical_and(paced, from_end == d)))
            def _():
                push(h, d).wait_recv()

    pltpu.make_async_copy(sums, sums, mate_send).wait()
    pltpu.make_async_copy(gathered, gathered, sum_send).wait()
    sent = stage.at[:, pl.ds(0, groups - 1)]
    pltpu.make_async_copy(sent, sent, out_send).wait()


def write_out(land, dq_hbm, dk_hbm, dv_hbm, write_sem):
    columns = land.shape[2]
    pieces = 4
    width = columns // pieces
    copies = []
    for c, ref in enumerate((dq_hbm, dk_hbm, dv_hbm)):
        for i in range(pieces):
            piece = pl.ds(i * width, width)
            copies.append(
                pltpu.make_async_copy(
                    land.at[c, :, piece], ref.at[:, piece], write_sem.at[c * pieces + i]
                )
            )
    for copy in copies:
        copy.start()
    for copy in copies:
        copy.wait()


def body(queries, keys, values, grad_out, rates, doc_lengths):
    length, columns = queries.shape
    heads = rates.shape[0]
    head_dim = columns // heads
    shards = lax.axis_size("seq")
    groups = lax.axis_size("head")
    part = length // groups
    docs = doc_lengths.shape[0]
    hbm = pl.BlockSpec(memory_space=pltpu.HBM)
    vmem = pl.BlockSpec(memory_space=pltpu.VMEM)
    bf16, f32 = jnp.bfloat16, jnp.float32
    landed = pl.pallas_call(
        functools.partial(kernel, shards, groups, docs),
        out_shape=pltpu.VMEM((3, part, groups * columns), bf16),
        in_specs=[hbm] * 6,
        out_specs=vmem,
        scratch_shapes=[
            pltpu.SMEM(doc_lengths.shape, jnp.int32),
            pltpu.SMEM(rates.shape, f32),
            pltpu.VMEM((heads, 4, length, head_dim), bf16),
            pltpu.VMEM((length, length), f32),
            pltpu.VMEM((length, length), f32),
            pltpu.VMEM((4, length, head_dim), f32),
            pltpu.VMEM((heads, 2, head_dim, head_dim), f32),
            pltpu.VMEM((heads, 2, head_dim, head_dim), f32),
            pltpu.VMEM((heads, 2, head_dim // 2, head_dim), f32),
            pltpu.VMEM((heads, shards // 2 - 1, 2, head_dim // 2, head_dim), f32),
            pltpu.VMEM((3, length, head_dim), f32),
            pltpu.VMEM((heads, groups, 3, part, head_dim), bf16),
            pltpu.SMEM((2, shards // 2 + 2), f32),
            pltpu.SemaphoreType.DMA((heads,)),
            pltpu.SemaphoreType.DMA,
            pltpu.SemaphoreType.DMA((heads,)),
            pltpu.SemaphoreType.DMA,
            pltpu.SemaphoreType.DMA((heads,)),
            pltpu.SemaphoreType.DMA,
            pltpu.SemaphoreType.DMA((groups - 1, heads)),
            pltpu.SemaphoreType.DMA((2,)),
        ],
        compiler_params=pltpu.CompilerParams(
            collective_id=0, has_side_effects=True, vmem_limit_bytes=VMEM_BYTES - 6 * part * groups * columns
        ),
        cost_estimate=pl.CostEstimate(
            flops=heads * length * (10 * length + 10 * head_dim) * head_dim,
            bytes_accessed=7 * length * columns * 2,
            transcendentals=heads * length * (length + 4 * head_dim),
        ),
    )(doc_lengths, rates, queries, keys, values, grad_out)
    out = jax.ShapeDtypeStruct((part, groups * columns), bf16)
    return pl.pallas_call(
        write_out,
        out_shape=(out, out, out),
        in_specs=[pl.BlockSpec(memory_space=pl.ANY)],
        out_specs=(hbm, hbm, hbm),
        scratch_shapes=[pltpu.SemaphoreType.DMA((12,))],
        compiler_params=pltpu.CompilerParams(vmem_limit_bytes=1024 * 1024),
    )(landed)


def solution(mesh):
    return jax.shard_map(
        body,
        mesh=mesh,
        in_specs=(
            P("seq", "head"),
            P("seq", "head"),
            P("seq", "head"),
            P("seq", "head"),
            P("head"),
            P(),
        ),
        out_specs=(P(("seq", "head"), None), P(("seq", "head"), None), P(("seq", "head"), None)),
        check_vma=False,
    )
```

```python
import functools

import jax
import jax.numpy as jnp
from jax import lax
from jax.experimental import pallas as pl
from jax.experimental.pallas import tpu as pltpu
from jax.sharding import PartitionSpec as P

MESH = pl.DeviceIdType.MESH
NEVER = 1e30
VMEM_BYTES = 62 * 1024 * 1024


def dot(a, b, dims):
    return lax.dot_general(a, b, (dims, ((), ())), preferred_element_type=jnp.float32)


NN = ((1,), (0,))
NT = ((1,), (1,))
TN = ((0,), (0,))


def kernel(
    shards,
    groups,
    docs,
    lengths_hbm,
    rates_hbm,
    q_hbm,
    k_hbm,
    v_hbm,
    g_hbm,
    land,
    lengths,
    rates,
    rows_in,
    dist,
    dist_t,
    row_dist,
    sums,
    mates,
    pair_sums,
    gathered,
    acc,
    stage,
    arrived,
    gaps,
    load_sem,
    mate_send,
    mate_recv,
    sum_send,
    sum_recv,
    out_send,
    out_recv,
    small_sem,
):
    heads, _, length, head_dim = rows_in.shape
    part = length // groups
    shard = lax.axis_index("seq")
    group = lax.axis_index("head")
    pairs, pair, core = shards // 2, shard // 2, lax.rem(shard, 2)
    inputs = (q_hbm, k_hbm, v_hbm, g_hbm)

    def load(h):
        columns = pl.ds(pl.multiple_of(h * head_dim, head_dim), head_dim)
        return [
            pltpu.make_async_copy(ref.at[:, columns], rows_in.at[h, i], load_sem.at[h])
            for i, ref in enumerate(inputs)
        ]

    small = [
        pltpu.make_async_copy(lengths_hbm, lengths, small_sem.at[0]),
        pltpu.make_async_copy(rates_hbm, rates, small_sem.at[1]),
    ]
    for copy in small + load(0) + load(1):
        copy.start()

    barrier = pltpu.get_barrier_semaphore()
    for d in range(1, shards):
        peer = lax.rem(shard + d, shards)
        pl.semaphore_signal(barrier, inc=1, device_id=(peer, group), device_id_type=MESH)
    for d in range(1, groups):
        peer = lax.rem(group + d, groups)
        pl.semaphore_signal(barrier, inc=1, device_id=(shard, peer), device_id_type=MESH)

    first = shard * length
    for copy in small:
        copy.wait()

    def starts():
        total = jnp.int32(0)
        for i in range(docs):
            yield total
            total = total + lengths[i]

    def seg(positions):
        count = -1
        for start in starts():
            count = count + jnp.where(start <= positions, 1, 0)
        return count

    seg_first = seg(first)
    seg_last = seg(first + length - 1)
    seg_prev = seg(first - 1)
    seg_next = seg(first + length)
    wide = (length, head_dim)
    offset = lax.broadcasted_iota(jnp.int32, wide, 0)
    segment = seg(first + offset)
    where = offset.astype(jnp.float32)
    row_dist[0] = jnp.where(segment == seg_last, length - 1.0 - where, NEVER)
    row_dist[1] = jnp.where(segment == seg_first, where, NEVER)

    def summarise(h):
        pltpu.make_async_copy(rows_in.at[h], rows_in.at[h], load_sem.at[h]).wait()
        rate = rates[h]
        weighted_k = (
            rows_in[h, 1].astype(jnp.float32) * jnp.exp(-rate * row_dist[0])
        ).astype(jnp.bfloat16)
        sums[h, 0] = dot(weighted_k, rows_in[h, 2], TN)
        weighted_q = (
            rows_in[h, 0].astype(jnp.float32) * jnp.exp(-rate * row_dist[1])
        ).astype(jnp.bfloat16)
        sums[h, 1] = dot(weighted_q, rows_in[h, 3], TN)

    def swap(h):
        return pltpu.make_async_remote_copy(
            src_ref=sums.at[h],
            dst_ref=mates.at[h],
            send_sem=mate_send,
            recv_sem=mate_recv.at[h],
            device_id=(pair * 2 + 1 - core, group),
            device_id_type=MESH,
        )

    def factor(way, entry, rate):
        return jnp.exp(jnp.full((1, head_dim), -rate * gaps[way, entry]))

    def send_sums(h):
        swap(h).wait_recv()
        rate = rates[h]
        half = pl.ds(pl.multiple_of(core * (head_dim // 2), head_dim // 2), head_dim // 2)
        for way in range(2):
            pair_sums[h, way] = (
                factor(way, pairs, rate) * sums[h, way, half]
                + factor(way, pairs + 1, rate) * mates[h, way, half]
            )
        for d in range(1, pairs):
            peer = lax.rem(pair + d, pairs)
            back = (pair + d) // pairs
            for side in range(2):
                pltpu.make_async_remote_copy(
                    src_ref=pair_sums.at[h, back],
                    dst_ref=gathered.at[h, d - 1, core],
                    send_sem=sum_send,
                    recv_sem=sum_recv.at[h],
                    device_id=(peer * 2 + side, group),
                    device_id_type=MESH,
                ).start()

    summarise(0)

    row_dist[2] = jnp.where(segment == seg_prev, where + 1.0, NEVER)
    row_dist[3] = jnp.where(segment == seg_next, length - where, NEVER)

    tile = min(256, length)
    tiles = length // tile
    across = lax.broadcasted_iota(jnp.int32, (1, length), 1)
    seg_across = seg(first + across)
    for i in range(tiles):
        down = i * tile + lax.broadcasted_iota(jnp.int32, (tile, 1), 0)
        seg_down = seg(first + down)
        gap = down - across
        dist[pl.ds(i * tile, tile), :] = jnp.where(
            jnp.logical_and(seg_down == seg_across, gap >= 0), gap.astype(jnp.float32), NEVER
        )
        dist_t[pl.ds(i * tile, tile), :] = jnp.where(
            jnp.logical_and(seg_down == seg_across, gap <= 0), -gap.astype(jnp.float32), NEVER
        )

    for d in range(1, pairs):
        source = lax.rem(pair - d + pairs, pairs)
        ahead = (pair + pairs - d) // pairs
        same_fwd = seg((source + 1) * 2 * length - 1) == seg_prev
        same_bwd = seg(source * 2 * length) == seg_next
        gap_fwd = (2 * (d - 1) + core) * length
        gap_bwd = (2 * (pairs - d) - 1 - core) * length
        gaps[0, d - 1] = jnp.where(
            jnp.logical_and(ahead == 1, same_fwd), gap_fwd.astype(jnp.float32), NEVER
        )
        gaps[1, d - 1] = jnp.where(
            jnp.logical_and(ahead == 0, same_bwd), gap_bwd.astype(jnp.float32), NEVER
        )
    left = pair * 2 * length
    kept_fwd = seg(left + 2 * length - 1) == seg(left + length - 1)
    kept_bwd = seg(left) == seg(left + length)
    step_fwd = jnp.where(kept_fwd, float(length), NEVER)
    step_bwd = jnp.where(kept_bwd, float(length), NEVER)
    is_left = core == 0
    gaps[0, pairs - 1] = jnp.where(is_left, NEVER, 0.0)
    gaps[1, pairs - 1] = jnp.where(is_left, 0.0, NEVER)
    gaps[0, pairs] = jnp.where(is_left, step_fwd, 0.0)
    gaps[0, pairs + 1] = jnp.where(is_left, 0.0, step_fwd)
    gaps[1, pairs] = jnp.where(is_left, 0.0, step_bwd)
    gaps[1, pairs + 1] = jnp.where(is_left, step_bwd, 0.0)

    pl.semaphore_wait(barrier, shards + groups - 2)
    swap(0).start()
    summarise(1)
    swap(1).start()
    send_sums(0)

    order = sorted(range(1, groups), key=lambda d: abs(2 * d - groups))

    def columns_of(source, h):
        return pl.ds(pl.multiple_of((source * heads + h) * head_dim, head_dim), head_dim)

    def push(h, d):
        peer = lax.rem(group + d, groups)
        return pltpu.make_async_remote_copy(
            src_ref=stage.at[h, peer],
            dst_ref=arrived.at[h, d - 1],
            send_sem=out_send,
            recv_sem=out_recv.at[d - 1, h],
            device_id=(shard, peer),
            device_id_type=MESH,
        )

    @pl.loop(0, heads)
    def _(h):
        @pl.when(h + 2 < heads)
        def _():
            for copy in load(h + 2):
                copy.start()

        rate = rates[h]
        for i in range(tiles):
            rows = pl.ds(i * tile, tile)
            seen = pl.ds(0, (i + 1) * tile)
            later = pl.ds(i * tile, length - i * tile)
            decay = jnp.exp(-rate * dist[rows, seen])
            p = decay * dot(rows_in[h, 3, rows], rows_in[h, 2, seen], NT)
            acc[0, rows] = dot(p.astype(jnp.bfloat16), rows_in[h, 1, seen], NN)
            decay_t = jnp.exp(-rate * dist_t[rows, later])
            p_t = decay_t * dot(rows_in[h, 2, rows], rows_in[h, 3, later], NT)
            acc[1, rows] = dot(p_t.astype(jnp.bfloat16), rows_in[h, 0, later], NN)
            a_t = decay_t * dot(rows_in[h, 1, rows], rows_in[h, 0, later], NT)
            acc[2, rows] = dot(a_t.astype(jnp.bfloat16), rows_in[h, 3, later], NN)

        @pl.when(h + 1 < heads)
        def _():
            send_sums(h + 1)

        @pl.when(h + 2 < heads)
        def _():
            summarise(h + 2)
            swap(h + 2).start()

        pltpu.make_async_copy(gathered.at[h], gathered.at[h], sum_recv.at[h]).wait()
        state = factor(0, pairs - 1, rate) * mates[h, 0]
        back = factor(1, pairs - 1, rate) * mates[h, 1]
        for d in range(pairs - 1):
            summary = gathered[h, d].reshape(head_dim, head_dim)
            state += factor(0, d, rate) * summary
            back += factor(1, d, rate) * summary
        state = state.astype(jnp.bfloat16)
        back = back.astype(jnp.bfloat16)
        factor_in = jnp.exp(-rate * row_dist[2])
        factor_back = jnp.exp(-rate * row_dist[3])
        dq = acc[0] + dot(rows_in[h, 3], state, NT) * factor_in
        dk = acc[1] + dot(rows_in[h, 2], back, NT) * factor_back
        dv = acc[2] + dot(rows_in[h, 1], back, NN) * factor_back
        for c, total in enumerate((dq, dk, dv)):
            stage[h, :, c] = total.astype(jnp.bfloat16).reshape(groups, part, head_dim)
        for d in order:
            push(h, d).start()
        land[:, :, columns_of(group, h)] = stage[h, group]

    @pl.loop(0, heads)
    def _(h):
        for d in order:
            push(h, d).wait_recv()
            source = lax.rem(group - d + groups, groups)
            land[:, :, columns_of(source, h)] = arrived[h, d - 1]

    pltpu.make_async_copy(sums, sums, mate_send).wait()
    pltpu.make_async_copy(gathered, gathered, sum_send).wait()
    pltpu.make_async_copy(arrived, arrived, out_send).wait()


def write_out(land, dq_hbm, dk_hbm, dv_hbm, write_sem):
    columns = land.shape[2]
    pieces = 4
    width = columns // pieces
    copies = []
    for c, ref in enumerate((dq_hbm, dk_hbm, dv_hbm)):
        for i in range(pieces):
            piece = pl.ds(i * width, width)
            copies.append(
                pltpu.make_async_copy(
                    land.at[c, :, piece], ref.at[:, piece], write_sem.at[c * pieces + i]
                )
            )
    for copy in copies:
        copy.start()
    for copy in copies:
        copy.wait()


def body(queries, keys, values, grad_out, rates, doc_lengths):
    length, columns = queries.shape
    heads = rates.shape[0]
    head_dim = columns // heads
    shards = lax.axis_size("seq")
    groups = lax.axis_size("head")
    part = length // groups
    docs = doc_lengths.shape[0]
    hbm = pl.BlockSpec(memory_space=pltpu.HBM)
    vmem = pl.BlockSpec(memory_space=pltpu.VMEM)
    bf16, f32 = jnp.bfloat16, jnp.float32
    landed = pl.pallas_call(
        functools.partial(kernel, shards, groups, docs),
        out_shape=pltpu.VMEM((3, part, groups * columns), bf16),
        in_specs=[hbm] * 6,
        out_specs=vmem,
        scratch_shapes=[
            pltpu.SMEM(doc_lengths.shape, jnp.int32),
            pltpu.SMEM(rates.shape, f32),
            pltpu.VMEM((heads, 4, length, head_dim), bf16),
            pltpu.VMEM((length, length), f32),
            pltpu.VMEM((length, length), f32),
            pltpu.VMEM((4, length, head_dim), f32),
            pltpu.VMEM((heads, 2, head_dim, head_dim), f32),
            pltpu.VMEM((heads, 2, head_dim, head_dim), f32),
            pltpu.VMEM((heads, 2, head_dim // 2, head_dim), f32),
            pltpu.VMEM((heads, shards // 2 - 1, 2, head_dim // 2, head_dim), f32),
            pltpu.VMEM((3, length, head_dim), f32),
            pltpu.VMEM((heads, groups, 3, part, head_dim), bf16),
            pltpu.VMEM((heads, groups - 1, 3, part, head_dim), bf16),
            pltpu.SMEM((2, shards // 2 + 2), f32),
            pltpu.SemaphoreType.DMA((heads,)),
            pltpu.SemaphoreType.DMA,
            pltpu.SemaphoreType.DMA((heads,)),
            pltpu.SemaphoreType.DMA,
            pltpu.SemaphoreType.DMA((heads,)),
            pltpu.SemaphoreType.DMA,
            pltpu.SemaphoreType.DMA((groups - 1, heads)),
            pltpu.SemaphoreType.DMA((2,)),
        ],
        compiler_params=pltpu.CompilerParams(
            collective_id=0, has_side_effects=True, vmem_limit_bytes=VMEM_BYTES - 6 * part * groups * columns
        ),
        cost_estimate=pl.CostEstimate(
            flops=heads * length * (10 * length + 10 * head_dim) * head_dim,
            bytes_accessed=7 * length * columns * 2,
            transcendentals=heads * length * (length + 4 * head_dim),
        ),
    )(doc_lengths, rates, queries, keys, values, grad_out)
    out = jax.ShapeDtypeStruct((part, groups * columns), bf16)
    return pl.pallas_call(
        write_out,
        out_shape=(out, out, out),
        in_specs=[pl.BlockSpec(memory_space=pl.ANY)],
        out_specs=(hbm, hbm, hbm),
        scratch_shapes=[pltpu.SemaphoreType.DMA((12,))],
        compiler_params=pltpu.CompilerParams(vmem_limit_bytes=1024 * 1024),
    )(landed)


def solution(mesh):
    return jax.shard_map(
        body,
        mesh=mesh,
        in_specs=(
            P("seq", "head"),
            P("seq", "head"),
            P("seq", "head"),
            P("seq", "head"),
            P("head"),
            P(),
        ),
        out_specs=(P(("seq", "head"), None), P(("seq", "head"), None), P(("seq", "head"), None)),
        check_vma=False,
    )
```

```python
import functools

import jax
import jax.numpy as jnp
from jax import lax
from jax.experimental import pallas as pl
from jax.experimental.pallas import tpu as pltpu
from jax.sharding import PartitionSpec as P

MESH = pl.DeviceIdType.MESH
NEVER = 1e30
VMEM_BYTES = 62 * 1024 * 1024


def dot(a, b, dims):
    return lax.dot_general(a, b, (dims, ((), ())), preferred_element_type=jnp.float32)


NN = ((1,), (0,))
NT = ((1,), (1,))
TN = ((0,), (0,))


def kernel(
    shards,
    groups,
    docs,
    lengths_hbm,
    rates_hbm,
    q_hbm,
    k_hbm,
    v_hbm,
    g_hbm,
    land,
    lengths,
    rates,
    rows_in,
    dist,
    dist_t,
    row_dist,
    sums,
    mates,
    pair_sums,
    gathered,
    acc,
    stage,
    gaps,
    load_sem,
    mate_send,
    mate_recv,
    sum_send,
    sum_recv,
    out_send,
    out_recv,
    small_sem,
):
    heads, _, length, head_dim = rows_in.shape
    part = length // groups
    shard = lax.axis_index("seq")
    group = lax.axis_index("head")
    pairs, pair, core = shards // 2, shard // 2, lax.rem(shard, 2)
    inputs = (q_hbm, k_hbm, v_hbm, g_hbm)

    def load(h):
        columns = pl.ds(pl.multiple_of(h * head_dim, head_dim), head_dim)
        return [
            pltpu.make_async_copy(ref.at[:, columns], rows_in.at[h, i], load_sem.at[h])
            for i, ref in enumerate(inputs)
        ]

    barrier = pltpu.get_barrier_semaphore()
    for d in range(1, groups):
        peer = lax.rem(group + d, groups)
        pl.semaphore_signal(barrier, inc=1, device_id=(shard, peer), device_id_type=MESH)
    for d in range(1, shards):
        peer = lax.rem(shard + d, shards)
        pl.semaphore_signal(barrier, inc=1, device_id=(peer, group), device_id_type=MESH)

    small = [
        pltpu.make_async_copy(lengths_hbm, lengths, small_sem.at[0]),
        pltpu.make_async_copy(rates_hbm, rates, small_sem.at[1]),
    ]
    for copy in small + load(0) + load(1):
        copy.start()

    first = shard * length
    for copy in small:
        copy.wait()

    def starts():
        total = jnp.int32(0)
        for i in range(docs):
            yield total
            total = total + lengths[i]

    def seg(positions):
        count = -1
        for start in starts():
            count = count + jnp.where(start <= positions, 1, 0)
        return count

    seg_first = seg(first)
    seg_last = seg(first + length - 1)
    seg_prev = seg(first - 1)
    seg_next = seg(first + length)
    wide = (length, head_dim)
    offset = lax.broadcasted_iota(jnp.int32, wide, 0)
    segment = seg(first + offset)
    where = offset.astype(jnp.float32)
    row_dist[0] = jnp.where(segment == seg_last, length - 1.0 - where, NEVER)
    row_dist[1] = jnp.where(segment == seg_first, where, NEVER)

    def summarise(h):
        pltpu.make_async_copy(rows_in.at[h], rows_in.at[h], load_sem.at[h]).wait()
        rate = rates[h]
        weighted_k = (
            rows_in[h, 1].astype(jnp.float32) * jnp.exp(-rate * row_dist[0])
        ).astype(jnp.bfloat16)
        sums[h, 0] = dot(weighted_k, rows_in[h, 2], TN)
        weighted_q = (
            rows_in[h, 0].astype(jnp.float32) * jnp.exp(-rate * row_dist[1])
        ).astype(jnp.bfloat16)
        sums[h, 1] = dot(weighted_q, rows_in[h, 3], TN)

    def swap(h):
        return pltpu.make_async_remote_copy(
            src_ref=sums.at[h],
            dst_ref=mates.at[h],
            send_sem=mate_send,
            recv_sem=mate_recv.at[h],
            device_id=(pair * 2 + 1 - core, group),
            device_id_type=MESH,
        )

    def factor(way, entry, rate):
        return jnp.exp(jnp.full((1, head_dim), -rate * gaps[way, entry]))

    def send_sums(h):
        swap(h).wait_recv()
        rate = rates[h]
        half = pl.ds(pl.multiple_of(core * (head_dim // 2), head_dim // 2), head_dim // 2)
        for way in range(2):
            pair_sums[h, way] = (
                factor(way, pairs, rate) * sums[h, way, half]
                + factor(way, pairs + 1, rate) * mates[h, way, half]
            )
        for d in range(1, pairs):
            peer = lax.rem(pair + d, pairs)
            back = (pair + d) // pairs
            for side in range(2):
                pltpu.make_async_remote_copy(
                    src_ref=pair_sums.at[h, back],
                    dst_ref=gathered.at[h, d - 1, core],
                    send_sem=sum_send,
                    recv_sem=sum_recv.at[h],
                    device_id=(peer * 2 + side, group),
                    device_id_type=MESH,
                ).start()

    summarise(0)

    row_dist[2] = jnp.where(segment == seg_prev, where + 1.0, NEVER)
    row_dist[3] = jnp.where(segment == seg_next, length - where, NEVER)

    tile = min(256, length)
    tiles = length // tile
    across = lax.broadcasted_iota(jnp.int32, (1, length), 1)
    seg_across = seg(first + across)
    for i in range(tiles):
        down = i * tile + lax.broadcasted_iota(jnp.int32, (tile, 1), 0)
        seg_down = seg(first + down)
        gap = down - across
        dist[pl.ds(i * tile, tile), :] = jnp.where(
            jnp.logical_and(seg_down == seg_across, gap >= 0), gap.astype(jnp.float32), NEVER
        )
        dist_t[pl.ds(i * tile, tile), :] = jnp.where(
            jnp.logical_and(seg_down == seg_across, gap <= 0), -gap.astype(jnp.float32), NEVER
        )

    for d in range(1, pairs):
        source = lax.rem(pair - d + pairs, pairs)
        ahead = (pair + pairs - d) // pairs
        same_fwd = seg((source + 1) * 2 * length - 1) == seg_prev
        same_bwd = seg(source * 2 * length) == seg_next
        gap_fwd = (2 * (d - 1) + core) * length
        gap_bwd = (2 * (pairs - d) - 1 - core) * length
        gaps[0, d - 1] = jnp.where(
            jnp.logical_and(ahead == 1, same_fwd), gap_fwd.astype(jnp.float32), NEVER
        )
        gaps[1, d - 1] = jnp.where(
            jnp.logical_and(ahead == 0, same_bwd), gap_bwd.astype(jnp.float32), NEVER
        )
    left = pair * 2 * length
    kept_fwd = seg(left + 2 * length - 1) == seg(left + length - 1)
    kept_bwd = seg(left) == seg(left + length)
    step_fwd = jnp.where(kept_fwd, float(length), NEVER)
    step_bwd = jnp.where(kept_bwd, float(length), NEVER)
    is_left = core == 0
    gaps[0, pairs - 1] = jnp.where(is_left, NEVER, 0.0)
    gaps[1, pairs - 1] = jnp.where(is_left, 0.0, NEVER)
    gaps[0, pairs] = jnp.where(is_left, step_fwd, 0.0)
    gaps[0, pairs + 1] = jnp.where(is_left, 0.0, step_fwd)
    gaps[1, pairs] = jnp.where(is_left, 0.0, step_bwd)
    gaps[1, pairs + 1] = jnp.where(is_left, step_bwd, 0.0)

    pl.semaphore_wait(barrier, shards + groups - 2)
    swap(0).start()
    summarise(1)
    swap(1).start()
    send_sums(0)

    order = sorted(range(1, groups), key=lambda d: abs(2 * d - groups))

    def columns_of(source, h):
        return pl.ds(pl.multiple_of((source * heads + h) * head_dim, head_dim), head_dim)

    def push(h, d, which=pl.ds(0, 3)):
        peer = lax.rem(group + d, groups)
        return pltpu.make_async_remote_copy(
            src_ref=stage.at[h, peer, which],
            dst_ref=land.at[which, :, columns_of(group, h)],
            send_sem=out_send,
            recv_sem=out_recv.at[d - 1, h],
            device_id=(shard, peer),
            device_id_type=MESH,
        )

    @pl.loop(0, heads)
    def _(h):
        @pl.when(h + 2 < heads)
        def _():
            for copy in load(h + 2):
                copy.start()

        rate = rates[h]
        for i in range(tiles):
            rows = pl.ds(i * tile, tile)
            seen = pl.ds(0, (i + 1) * tile)
            later = pl.ds(i * tile, length - i * tile)
            decay = jnp.exp(-rate * dist[rows, seen])
            p = decay * dot(rows_in[h, 3, rows], rows_in[h, 2, seen], NT)
            acc[0, rows] = dot(p.astype(jnp.bfloat16), rows_in[h, 1, seen], NN)
            decay_t = jnp.exp(-rate * dist_t[rows, later])
            p_t = decay_t * dot(rows_in[h, 2, rows], rows_in[h, 3, later], NT)
            acc[1, rows] = dot(p_t.astype(jnp.bfloat16), rows_in[h, 0, later], NN)
            a_t = decay_t * dot(rows_in[h, 1, rows], rows_in[h, 0, later], NT)
            acc[2, rows] = dot(a_t.astype(jnp.bfloat16), rows_in[h, 3, later], NN)

        @pl.when(h + 1 < heads)
        def _():
            send_sums(h + 1)

        @pl.when(h + 2 < heads)
        def _():
            summarise(h + 2)
            swap(h + 2).start()

        pltpu.make_async_copy(gathered.at[h], gathered.at[h], sum_recv.at[h]).wait()
        def state_of(way):
            total = factor(way, pairs - 1, rate) * mates[h, way]
            for d in range(pairs - 1):
                total += factor(way, d, rate) * gathered[h, d].reshape(head_dim, head_dim)
            return total.astype(jnp.bfloat16)

        def finish(c, outer):
            total = (acc[c] + outer).astype(jnp.bfloat16)
            stage[h, :, c] = total.reshape(groups, part, head_dim)
            for d in order:
                push(h, d, pl.ds(c, 1)).start()

        state = state_of(0)
        finish(0, dot(rows_in[h, 3], state, NT) * jnp.exp(-rate * row_dist[2]))
        back = state_of(1)
        factor_back = jnp.exp(-rate * row_dist[3])
        finish(1, dot(rows_in[h, 2], back, NT) * factor_back)
        finish(2, dot(rows_in[h, 1], back, NN) * factor_back)
        land[:, :, columns_of(group, h)] = stage[h, group]

    @pl.loop(0, heads)
    def _(h):
        for d in order:
            push(h, d).wait_recv()

    pltpu.make_async_copy(sums, sums, mate_send).wait()
    pltpu.make_async_copy(gathered, gathered, sum_send).wait()
    sent = stage.at[:, pl.ds(0, groups - 1)]
    pltpu.make_async_copy(sent, sent, out_send).wait()


def write_out(land, dq_hbm, dk_hbm, dv_hbm, write_sem):
    rows = land.shape[1]
    band = min(32, rows)
    copies = []
    for c, ref in enumerate((dq_hbm, dk_hbm, dv_hbm)):
        for i in range(rows // band):
            piece = pl.ds(i * band, band)
            copies.append(
                pltpu.make_async_copy(
                    land.at[c, piece], ref.at[piece], write_sem.at[c, i]
                )
            )
    for copy in copies:
        copy.start()
    for copy in copies:
        copy.wait()


def body(queries, keys, values, grad_out, rates, doc_lengths):
    length, columns = queries.shape
    heads = rates.shape[0]
    head_dim = columns // heads
    shards = lax.axis_size("seq")
    groups = lax.axis_size("head")
    part = length // groups
    docs = doc_lengths.shape[0]
    hbm = pl.BlockSpec(memory_space=pltpu.HBM)
    vmem = pl.BlockSpec(memory_space=pltpu.VMEM)
    bf16, f32 = jnp.bfloat16, jnp.float32
    landed = pl.pallas_call(
        functools.partial(kernel, shards, groups, docs),
        out_shape=pltpu.VMEM((3, part, groups * columns), bf16),
        in_specs=[hbm] * 6,
        out_specs=vmem,
        scratch_shapes=[
            pltpu.SMEM(doc_lengths.shape, jnp.int32),
            pltpu.SMEM(rates.shape, f32),
            pltpu.VMEM((heads, 4, length, head_dim), bf16),
            pltpu.VMEM((length, length), f32),
            pltpu.VMEM((length, length), f32),
            pltpu.VMEM((4, length, head_dim), f32),
            pltpu.VMEM((heads, 2, head_dim, head_dim), f32),
            pltpu.VMEM((heads, 2, head_dim, head_dim), f32),
            pltpu.VMEM((heads, 2, head_dim // 2, head_dim), f32),
            pltpu.VMEM((heads, shards // 2 - 1, 2, head_dim // 2, head_dim), f32),
            pltpu.VMEM((3, length, head_dim), f32),
            pltpu.VMEM((heads, groups, 3, part, head_dim), bf16),
            pltpu.SMEM((2, shards // 2 + 2), f32),
            pltpu.SemaphoreType.DMA((heads,)),
            pltpu.SemaphoreType.DMA,
            pltpu.SemaphoreType.DMA((heads,)),
            pltpu.SemaphoreType.DMA,
            pltpu.SemaphoreType.DMA((heads,)),
            pltpu.SemaphoreType.DMA,
            pltpu.SemaphoreType.DMA((groups - 1, heads)),
            pltpu.SemaphoreType.DMA((2,)),
        ],
        compiler_params=pltpu.CompilerParams(
            collective_id=0, has_side_effects=True, vmem_limit_bytes=VMEM_BYTES - 6 * part * groups * columns
        ),
        cost_estimate=pl.CostEstimate(
            flops=heads * length * (10 * length + 10 * head_dim) * head_dim,
            bytes_accessed=7 * length * columns * 2,
            transcendentals=heads * length * (length + 4 * head_dim),
        ),
    )(doc_lengths, rates, queries, keys, values, grad_out)
    out = jax.ShapeDtypeStruct((part, groups * columns), bf16)
    return pl.pallas_call(
        write_out,
        out_shape=(out, out, out),
        in_specs=[pl.BlockSpec(memory_space=pl.ANY)],
        out_specs=(hbm, hbm, hbm),
        scratch_shapes=[pltpu.SemaphoreType.DMA((3, part // min(32, part)))],
        compiler_params=pltpu.CompilerParams(vmem_limit_bytes=1024 * 1024),
    )(landed)


def solution(mesh):
    return jax.shard_map(
        body,
        mesh=mesh,
        in_specs=(
            P("seq", "head"),
            P("seq", "head"),
            P("seq", "head"),
            P("seq", "head"),
            P("head"),
            P(),
        ),
        out_specs=(P(("seq", "head"), None), P(("seq", "head"), None), P(("seq", "head"), None)),
        check_vma=False,
    )
```

```python
import functools

import jax
import jax.numpy as jnp
from jax import lax
from jax.experimental import pallas as pl
from jax.experimental.pallas import tpu as pltpu
from jax.sharding import PartitionSpec as P

MESH = pl.DeviceIdType.MESH
NEVER = 1e30
VMEM_BYTES = 62 * 1024 * 1024


def dot(a, b, dims):
    return lax.dot_general(a, b, (dims, ((), ())), preferred_element_type=jnp.float32)


NN = ((1,), (0,))
NT = ((1,), (1,))
TN = ((0,), (0,))


def kernel(
    shards,
    groups,
    docs,
    lengths_hbm,
    rates_hbm,
    q_hbm,
    k_hbm,
    v_hbm,
    g_hbm,
    land,
    lengths,
    rates,
    rows_in,
    dist,
    row_dist,
    sums,
    mates,
    pair_sums,
    gathered,
    acc,
    stage,
    gaps,
    load_sem,
    mate_send,
    mate_recv,
    sum_send,
    sum_recv,
    out_send,
    out_recv,
    small_sem,
):
    heads, _, length, head_dim = rows_in.shape
    part = length // groups
    shard = lax.axis_index("seq")
    group = lax.axis_index("head")
    pairs, pair, core = shards // 2, shard // 2, lax.rem(shard, 2)
    inputs = (q_hbm, k_hbm, v_hbm, g_hbm)

    def load(h):
        columns = pl.ds(pl.multiple_of(h * head_dim, head_dim), head_dim)
        return [
            pltpu.make_async_copy(ref.at[:, columns], rows_in.at[h, i], load_sem.at[h])
            for i, ref in enumerate(inputs)
        ]

    small = [
        pltpu.make_async_copy(lengths_hbm, lengths, small_sem.at[0]),
        pltpu.make_async_copy(rates_hbm, rates, small_sem.at[1]),
    ]
    for copy in small + load(0) + load(1):
        copy.start()

    barrier = pltpu.get_barrier_semaphore()
    for d in range(1, shards):
        peer = lax.rem(shard + d, shards)
        pl.semaphore_signal(barrier, inc=1, device_id=(peer, group), device_id_type=MESH)
    for d in range(1, groups):
        peer = lax.rem(group + d, groups)
        pl.semaphore_signal(barrier, inc=1, device_id=(shard, peer), device_id_type=MESH)

    first = shard * length
    for copy in small:
        copy.wait()

    def starts():
        total = jnp.int32(0)
        for i in range(docs):
            yield total
            total = total + lengths[i]

    def seg(positions):
        count = -1
        for start in starts():
            count = count + jnp.where(start <= positions, 1, 0)
        return count

    seg_first = seg(first)
    seg_last = seg(first + length - 1)
    seg_prev = seg(first - 1)
    seg_next = seg(first + length)
    wide = (length, head_dim)
    offset = lax.broadcasted_iota(jnp.int32, wide, 0)
    segment = seg(first + offset)
    where = offset.astype(jnp.float32)
    row_dist[0] = jnp.where(segment == seg_last, length - 1.0 - where, NEVER)
    row_dist[1] = jnp.where(segment == seg_first, where, NEVER)

    def summarise(h):
        pltpu.make_async_copy(rows_in.at[h], rows_in.at[h], load_sem.at[h]).wait()
        rate = rates[h]
        weighted_k = (
            rows_in[h, 1].astype(jnp.float32) * jnp.exp(-rate * row_dist[0])
        ).astype(jnp.bfloat16)
        sums[h, 0] = dot(weighted_k, rows_in[h, 2], TN)
        weighted_q = (
            rows_in[h, 0].astype(jnp.float32) * jnp.exp(-rate * row_dist[1])
        ).astype(jnp.bfloat16)
        sums[h, 1] = dot(weighted_q, rows_in[h, 3], TN)

    def swap(h):
        return pltpu.make_async_remote_copy(
            src_ref=sums.at[h],
            dst_ref=mates.at[h],
            send_sem=mate_send,
            recv_sem=mate_recv.at[h],
            device_id=(pair * 2 + 1 - core, group),
            device_id_type=MESH,
        )

    def factor(way, entry, rate):
        return jnp.exp(jnp.full((1, head_dim), -rate * gaps[way, entry]))

    def send_sums(h):
        swap(h).wait_recv()
        rate = rates[h]
        half = pl.ds(pl.multiple_of(core * (head_dim // 2), head_dim // 2), head_dim // 2)
        for way in range(2):
            pair_sums[h, way] = (
                factor(way, pairs, rate) * sums[h, way, half]
                + factor(way, pairs + 1, rate) * mates[h, way, half]
            )
        for d in range(1, pairs):
            peer = lax.rem(pair + d, pairs)
            back = (pair + d) // pairs
            for side in range(2):
                pltpu.make_async_remote_copy(
                    src_ref=pair_sums.at[h, back],
                    dst_ref=gathered.at[h, d - 1, core],
                    send_sem=sum_send,
                    recv_sem=sum_recv.at[h],
                    device_id=(peer * 2 + side, group),
                    device_id_type=MESH,
                ).start()

    summarise(0)

    row_dist[2] = jnp.where(segment == seg_prev, where + 1.0, NEVER)
    row_dist[3] = jnp.where(segment == seg_next, length - where, NEVER)

    tile = min(256, length)
    tiles = length // tile
    across = lax.broadcasted_iota(jnp.int32, (1, length), 1)
    seg_across = seg(first + across)
    for i in range(tiles):
        down = i * tile + lax.broadcasted_iota(jnp.int32, (tile, 1), 0)
        seg_down = seg(first + down)
        gap = down - across
        dist[pl.ds(i * tile, tile), :] = jnp.where(
            jnp.logical_and(seg_down == seg_across, gap >= 0), gap.astype(jnp.float32), NEVER
        )

    for d in range(1, pairs):
        source = lax.rem(pair - d + pairs, pairs)
        ahead = (pair + pairs - d) // pairs
        same_fwd = seg((source + 1) * 2 * length - 1) == seg_prev
        same_bwd = seg(source * 2 * length) == seg_next
        gap_fwd = (2 * (d - 1) + core) * length
        gap_bwd = (2 * (pairs - d) - 1 - core) * length
        gaps[0, d - 1] = jnp.where(
            jnp.logical_and(ahead == 1, same_fwd), gap_fwd.astype(jnp.float32), NEVER
        )
        gaps[1, d - 1] = jnp.where(
            jnp.logical_and(ahead == 0, same_bwd), gap_bwd.astype(jnp.float32), NEVER
        )
    left = pair * 2 * length
    kept_fwd = seg(left + 2 * length - 1) == seg(left + length - 1)
    kept_bwd = seg(left) == seg(left + length)
    step_fwd = jnp.where(kept_fwd, float(length), NEVER)
    step_bwd = jnp.where(kept_bwd, float(length), NEVER)
    is_left = core == 0
    gaps[0, pairs - 1] = jnp.where(is_left, NEVER, 0.0)
    gaps[1, pairs - 1] = jnp.where(is_left, 0.0, NEVER)
    gaps[0, pairs] = jnp.where(is_left, step_fwd, 0.0)
    gaps[0, pairs + 1] = jnp.where(is_left, 0.0, step_fwd)
    gaps[1, pairs] = jnp.where(is_left, 0.0, step_bwd)
    gaps[1, pairs + 1] = jnp.where(is_left, step_bwd, 0.0)

    pl.semaphore_wait(barrier, shards + groups - 2)
    swap(0).start()
    summarise(1)
    swap(1).start()
    send_sums(0)

    order = sorted(range(1, groups), key=lambda d: abs(2 * d - groups))

    def columns_of(source, h):
        return pl.ds(pl.multiple_of((source * heads + h) * head_dim, head_dim), head_dim)

    bunch = stage.shape[-1] // head_dim
    bunches = heads // bunch

    def push(b, d):
        peer = lax.rem(group + d, groups)
        return pltpu.make_async_remote_copy(
            src_ref=stage.at[b, peer],
            dst_ref=land.at[:, :, pl.ds(
                pl.multiple_of((group * heads + b * bunch) * head_dim, head_dim), bunch * head_dim
            )],
            send_sem=out_send,
            recv_sem=out_recv.at[d - 1, b],
            device_id=(shard, peer),
            device_id_type=MESH,
        )

    @pl.loop(0, heads)
    def _(h):
        @pl.when(h + 2 < heads)
        def _():
            for copy in load(h + 2):
                copy.start()

        rate = rates[h]
        for i in range(tiles):
            rows, seen = pl.ds(i * tile, tile), (i + 1) * tile
            q, g = rows_in[h, 0, rows], rows_in[h, 3, rows]
            k, v = rows_in[h, 1, pl.ds(0, seen)], rows_in[h, 2, pl.ds(0, seen)]
            decay = jnp.exp(-rate * dist[rows, pl.ds(0, seen)])
            p = (decay * dot(g, v, NT)).astype(jnp.bfloat16)
            a = (decay * dot(q, k, NT)).astype(jnp.bfloat16)
            acc[0, rows] = dot(p, k, NN)
            dk, dv = dot(p, q, TN), dot(a, g, TN)
            if i:
                acc[1, pl.ds(0, i * tile)] += dk[: i * tile]
                acc[2, pl.ds(0, i * tile)] += dv[: i * tile]
            acc[1, rows] = dk[i * tile :]
            acc[2, rows] = dv[i * tile :]

        @pl.when(h + 1 < heads)
        def _():
            send_sums(h + 1)

        @pl.when(h + 2 < heads)
        def _():
            summarise(h + 2)
            swap(h + 2).start()

        pltpu.make_async_copy(gathered.at[h], gathered.at[h], sum_recv.at[h]).wait()
        state = factor(0, pairs - 1, rate) * mates[h, 0]
        back = factor(1, pairs - 1, rate) * mates[h, 1]
        for d in range(pairs - 1):
            summary = gathered[h, d].reshape(head_dim, head_dim)
            state += factor(0, d, rate) * summary
            back += factor(1, d, rate) * summary
        state = state.astype(jnp.bfloat16)
        back = back.astype(jnp.bfloat16)
        factor_in = jnp.exp(-rate * row_dist[2])
        factor_back = jnp.exp(-rate * row_dist[3])
        dq = acc[0] + dot(rows_in[h, 3], state, NT) * factor_in
        dk = acc[1] + dot(rows_in[h, 2], back, NT) * factor_back
        dv = acc[2] + dot(rows_in[h, 1], back, NN) * factor_back
        inside = pl.ds(pl.multiple_of(lax.rem(h, bunch) * head_dim, head_dim), head_dim)
        for c, total in enumerate((dq, dk, dv)):
            stage[h // bunch, :, c, :, inside] = total.astype(jnp.bfloat16).reshape(
                groups, part, head_dim
            )

        @pl.when(lax.rem(h, bunch) == bunch - 1)
        def _():
            for d in order:
                push(h // bunch, d).start()

        land[:, :, columns_of(group, h)] = stage[h // bunch, group, :, :, inside]

    @pl.loop(0, bunches)
    def _(b):
        for d in order:
            push(b, d).wait_recv()

    pltpu.make_async_copy(sums, sums, mate_send).wait()
    pltpu.make_async_copy(gathered, gathered, sum_send).wait()
    sent = stage.at[:, pl.ds(0, groups - 1)]
    pltpu.make_async_copy(sent, sent, out_send).wait()


def write_out(land, dq_hbm, dk_hbm, dv_hbm, write_sem):
    columns = land.shape[2]
    pieces = 4
    width = columns // pieces
    copies = []
    for c, ref in enumerate((dq_hbm, dk_hbm, dv_hbm)):
        for i in range(pieces):
            piece = pl.ds(i * width, width)
            copies.append(
                pltpu.make_async_copy(
                    land.at[c, :, piece], ref.at[:, piece], write_sem.at[c * pieces + i]
                )
            )
    for copy in copies:
        copy.start()
    for copy in copies:
        copy.wait()


def body(queries, keys, values, grad_out, rates, doc_lengths):
    length, columns = queries.shape
    heads = rates.shape[0]
    head_dim = columns // heads
    shards = lax.axis_size("seq")
    groups = lax.axis_size("head")
    part = length // groups
    bunch = 2 if heads % 2 == 0 else 1
    docs = doc_lengths.shape[0]
    hbm = pl.BlockSpec(memory_space=pltpu.HBM)
    vmem = pl.BlockSpec(memory_space=pltpu.VMEM)
    bf16, f32 = jnp.bfloat16, jnp.float32
    landed = pl.pallas_call(
        functools.partial(kernel, shards, groups, docs),
        out_shape=pltpu.VMEM((3, part, groups * columns), bf16),
        in_specs=[hbm] * 6,
        out_specs=vmem,
        scratch_shapes=[
            pltpu.SMEM(doc_lengths.shape, jnp.int32),
            pltpu.SMEM(rates.shape, f32),
            pltpu.VMEM((heads, 4, length, head_dim), bf16),
            pltpu.VMEM((length, length), f32),
            pltpu.VMEM((4, length, head_dim), f32),
            pltpu.VMEM((heads, 2, head_dim, head_dim), f32),
            pltpu.VMEM((heads, 2, head_dim, head_dim), f32),
            pltpu.VMEM((heads, 2, head_dim // 2, head_dim), f32),
            pltpu.VMEM((heads, shards // 2 - 1, 2, head_dim // 2, head_dim), f32),
            pltpu.VMEM((3, length, head_dim), f32),
            pltpu.VMEM((heads // bunch, groups, 3, part, bunch * head_dim), bf16),
            pltpu.SMEM((2, shards // 2 + 2), f32),
            pltpu.SemaphoreType.DMA((heads,)),
            pltpu.SemaphoreType.DMA,
            pltpu.SemaphoreType.DMA((heads,)),
            pltpu.SemaphoreType.DMA,
            pltpu.SemaphoreType.DMA((heads,)),
            pltpu.SemaphoreType.DMA,
            pltpu.SemaphoreType.DMA((groups - 1, heads // bunch)),
            pltpu.SemaphoreType.DMA((2,)),
        ],
        compiler_params=pltpu.CompilerParams(
            collective_id=0, has_side_effects=True, vmem_limit_bytes=VMEM_BYTES - 6 * part * groups * columns
        ),
        cost_estimate=pl.CostEstimate(
            flops=heads * length * (10 * length + 10 * head_dim) * head_dim,
            bytes_accessed=7 * length * columns * 2,
            transcendentals=heads * length * (length + 4 * head_dim),
        ),
    )(doc_lengths, rates, queries, keys, values, grad_out)
    out = jax.ShapeDtypeStruct((part, groups * columns), bf16)
    return pl.pallas_call(
        write_out,
        out_shape=(out, out, out),
        in_specs=[pl.BlockSpec(memory_space=pl.ANY)],
        out_specs=(hbm, hbm, hbm),
        scratch_shapes=[pltpu.SemaphoreType.DMA((12,))],
        compiler_params=pltpu.CompilerParams(vmem_limit_bytes=1024 * 1024),
    )(landed)


def solution(mesh):
    return jax.shard_map(
        body,
        mesh=mesh,
        in_specs=(
            P("seq", "head"),
            P("seq", "head"),
            P("seq", "head"),
            P("seq", "head"),
            P("head"),
            P(),
        ),
        out_specs=(P(("seq", "head"), None), P(("seq", "head"), None), P(("seq", "head"), None)),
        check_vma=False,
    )
```

```python
import functools

import jax
import jax.numpy as jnp
from jax import lax
from jax.experimental import pallas as pl
from jax.experimental.pallas import tpu as pltpu
from jax.sharding import PartitionSpec as P

MESH = pl.DeviceIdType.MESH
NEVER = 1e30
VMEM_BYTES = 62 * 1024 * 1024


def dot(a, b, dims):
    return lax.dot_general(a, b, (dims, ((), ())), preferred_element_type=jnp.float32)


NN = ((1,), (0,))
NT = ((1,), (1,))
TN = ((0,), (0,))


def kernel(
    shards,
    groups,
    docs,
    lengths_hbm,
    rates_hbm,
    q_hbm,
    k_hbm,
    v_hbm,
    g_hbm,
    land,
    lengths,
    rates,
    rows_in,
    dist,
    row_dist,
    sums,
    mates,
    pair_sums,
    gathered,
    acc,
    stage,
    gaps,
    load_sem,
    mate_send,
    mate_recv,
    sum_send,
    sum_recv,
    out_send,
    out_recv,
    small_sem,
):
    heads, _, length, head_dim = rows_in.shape
    part = length // groups
    shard = lax.axis_index("seq")
    group = lax.axis_index("head")
    pairs, pair, core = shards // 2, shard // 2, lax.rem(shard, 2)
    inputs = (q_hbm, k_hbm, v_hbm, g_hbm)

    def load(h):
        columns = pl.ds(pl.multiple_of(h * head_dim, head_dim), head_dim)
        return [
            pltpu.make_async_copy(ref.at[:, columns], rows_in.at[h, i], load_sem.at[h])
            for i, ref in enumerate(inputs)
        ]

    barrier = pltpu.get_barrier_semaphore()
    for d in range(1, shards):
        peer = lax.rem(shard + d, shards)
        pl.semaphore_signal(barrier, inc=1, device_id=(peer, group), device_id_type=MESH)
    for d in range(1, groups):
        peer = lax.rem(group + d, groups)
        pl.semaphore_signal(barrier, inc=1, device_id=(shard, peer), device_id_type=MESH)

    small = [
        pltpu.make_async_copy(lengths_hbm, lengths, small_sem.at[0]),
        pltpu.make_async_copy(rates_hbm, rates, small_sem.at[1]),
    ]
    for copy in small + load(0) + load(1):
        copy.start()

    first = shard * length
    for copy in small:
        copy.wait()

    def starts():
        total = jnp.int32(0)
        for i in range(docs):
            yield total
            total = total + lengths[i]

    def seg(positions):
        count = -1
        for start in starts():
            count = count + jnp.where(start <= positions, 1, 0)
        return count

    seg_first = seg(first)
    seg_last = seg(first + length - 1)
    seg_prev = seg(first - 1)
    seg_next = seg(first + length)
    wide = (length, head_dim)
    offset = lax.broadcasted_iota(jnp.int32, wide, 0)
    segment = seg(first + offset)
    where = offset.astype(jnp.float32)
    row_dist[0] = jnp.where(segment == seg_last, length - 1.0 - where, NEVER)
    row_dist[1] = jnp.where(segment == seg_first, where, NEVER)

    def summarise(h):
        pltpu.make_async_copy(rows_in.at[h], rows_in.at[h], load_sem.at[h]).wait()
        rate = rates[h]
        weighted_k = (
            rows_in[h, 1].astype(jnp.float32) * jnp.exp(-rate * row_dist[0])
        ).astype(jnp.bfloat16)
        sums[h, 0] = dot(weighted_k, rows_in[h, 2], TN)
        weighted_q = (
            rows_in[h, 0].astype(jnp.float32) * jnp.exp(-rate * row_dist[1])
        ).astype(jnp.bfloat16)
        sums[h, 1] = dot(weighted_q, rows_in[h, 3], TN)

    def swap(h):
        return pltpu.make_async_remote_copy(
            src_ref=sums.at[h],
            dst_ref=mates.at[h],
            send_sem=mate_send,
            recv_sem=mate_recv.at[h],
            device_id=(pair * 2 + 1 - core, group),
            device_id_type=MESH,
        )

    def factor(way, entry, rate):
        return jnp.exp(jnp.full((1, head_dim), -rate * gaps[way, entry]))

    def send_sums(h):
        swap(h).wait_recv()
        rate = rates[h]
        half = pl.ds(pl.multiple_of(core * (head_dim // 2), head_dim // 2), head_dim // 2)
        for way in range(2):
            pair_sums[h, way] = (
                factor(way, pairs, rate) * sums[h, way, half]
                + factor(way, pairs + 1, rate) * mates[h, way, half]
            )
        for d in range(1, pairs):
            peer = lax.rem(pair + d, pairs)
            back = (pair + d) // pairs
            for side in range(2):
                pltpu.make_async_remote_copy(
                    src_ref=pair_sums.at[h, back],
                    dst_ref=gathered.at[h, d - 1, core],
                    send_sem=sum_send,
                    recv_sem=sum_recv.at[h],
                    device_id=(peer * 2 + side, group),
                    device_id_type=MESH,
                ).start()

    summarise(0)
    pl.semaphore_wait(barrier, shards + groups - 2)
    swap(0).start()

    row_dist[2] = jnp.where(segment == seg_prev, where + 1.0, NEVER)
    row_dist[3] = jnp.where(segment == seg_next, length - where, NEVER)

    tile = min(256, length)
    tiles = length // tile
    across = lax.broadcasted_iota(jnp.int32, (1, length), 1)
    seg_across = seg(first + across)
    for i in range(tiles):
        down = i * tile + lax.broadcasted_iota(jnp.int32, (tile, 1), 0)
        seg_down = seg(first + down)
        gap = down - across
        dist[pl.ds(i * tile, tile), :] = jnp.where(
            jnp.logical_and(seg_down == seg_across, gap >= 0), gap.astype(jnp.float32), NEVER
        )

    for d in range(1, pairs):
        source = lax.rem(pair - d + pairs, pairs)
        ahead = (pair + pairs - d) // pairs
        same_fwd = seg((source + 1) * 2 * length - 1) == seg_prev
        same_bwd = seg(source * 2 * length) == seg_next
        gap_fwd = (2 * (d - 1) + core) * length
        gap_bwd = (2 * (pairs - d) - 1 - core) * length
        gaps[0, d - 1] = jnp.where(
            jnp.logical_and(ahead == 1, same_fwd), gap_fwd.astype(jnp.float32), NEVER
        )
        gaps[1, d - 1] = jnp.where(
            jnp.logical_and(ahead == 0, same_bwd), gap_bwd.astype(jnp.float32), NEVER
        )
    left = pair * 2 * length
    kept_fwd = seg(left + 2 * length - 1) == seg(left + length - 1)
    kept_bwd = seg(left) == seg(left + length)
    step_fwd = jnp.where(kept_fwd, float(length), NEVER)
    step_bwd = jnp.where(kept_bwd, float(length), NEVER)
    is_left = core == 0
    gaps[0, pairs - 1] = jnp.where(is_left, NEVER, 0.0)
    gaps[1, pairs - 1] = jnp.where(is_left, 0.0, NEVER)
    gaps[0, pairs] = jnp.where(is_left, step_fwd, 0.0)
    gaps[0, pairs + 1] = jnp.where(is_left, 0.0, step_fwd)
    gaps[1, pairs] = jnp.where(is_left, 0.0, step_bwd)
    gaps[1, pairs + 1] = jnp.where(is_left, step_bwd, 0.0)

    send_sums(0)
    summarise(1)
    swap(1).start()

    order = sorted(range(1, groups), key=lambda d: abs(2 * d - groups))

    def columns_of(source, h):
        return pl.ds(pl.multiple_of((source * heads + h) * head_dim, head_dim), head_dim)

    def push(h, d):
        peer = lax.rem(group + d, groups)
        return pltpu.make_async_remote_copy(
            src_ref=stage.at[h, peer],
            dst_ref=land.at[:, :, columns_of(group, h)],
            send_sem=out_send,
            recv_sem=out_recv.at[d - 1, h],
            device_id=(shard, peer),
            device_id_type=MESH,
        )

    @pl.loop(0, heads)
    def _(h):
        @pl.when(h + 2 < heads)
        def _():
            for copy in load(h + 2):
                copy.start()

        rate = rates[h]
        for i in range(tiles):
            rows, seen = pl.ds(i * tile, tile), (i + 1) * tile
            q, g = rows_in[h, 0, rows], rows_in[h, 3, rows]
            k, v = rows_in[h, 1, pl.ds(0, seen)], rows_in[h, 2, pl.ds(0, seen)]
            decay = jnp.exp(-rate * dist[rows, pl.ds(0, seen)])
            p = (decay * dot(g, v, NT)).astype(jnp.bfloat16)
            a = (decay * dot(q, k, NT)).astype(jnp.bfloat16)
            acc[0, rows] = dot(p, k, NN)
            dk, dv = dot(p, q, TN), dot(a, g, TN)
            if i:
                acc[1, pl.ds(0, i * tile)] += dk[: i * tile]
                acc[2, pl.ds(0, i * tile)] += dv[: i * tile]
            acc[1, rows] = dk[i * tile :]
            acc[2, rows] = dv[i * tile :]

        @pl.when(h + 1 < heads)
        def _():
            send_sums(h + 1)

        @pl.when(h + 2 < heads)
        def _():
            summarise(h + 2)
            swap(h + 2).start()

        pltpu.make_async_copy(gathered.at[h], gathered.at[h], sum_recv.at[h]).wait()
        state = factor(0, pairs - 1, rate) * mates[h, 0]
        back = factor(1, pairs - 1, rate) * mates[h, 1]
        for d in range(pairs - 1):
            summary = gathered[h, d].reshape(head_dim, head_dim)
            state += factor(0, d, rate) * summary
            back += factor(1, d, rate) * summary
        state = state.astype(jnp.bfloat16)
        back = back.astype(jnp.bfloat16)
        factor_in = jnp.exp(-rate * row_dist[2])
        factor_back = jnp.exp(-rate * row_dist[3])
        dq = acc[0] + dot(rows_in[h, 3], state, NT) * factor_in
        dk = acc[1] + dot(rows_in[h, 2], back, NT) * factor_back
        dv = acc[2] + dot(rows_in[h, 1], back, NN) * factor_back
        for c, total in enumerate((dq, dk, dv)):
            stage[h, :, c] = total.astype(jnp.bfloat16).reshape(groups, part, head_dim)
        for d in order:
            push(h, d).start()
        land[:, :, columns_of(group, h)] = stage[h, group]

    @pl.loop(0, heads)
    def _(h):
        for d in order:
            push(h, d).wait_recv()

    pltpu.make_async_copy(sums, sums, mate_send).wait()
    pltpu.make_async_copy(gathered, gathered, sum_send).wait()
    sent = stage.at[:, pl.ds(0, groups - 1)]
    pltpu.make_async_copy(sent, sent, out_send).wait()


def write_out(land, dq_hbm, dk_hbm, dv_hbm, write_sem):
    columns = land.shape[2]
    pieces = 4
    width = columns // pieces
    copies = []
    for c, ref in enumerate((dq_hbm, dk_hbm, dv_hbm)):
        for i in range(pieces):
            piece = pl.ds(i * width, width)
            copies.append(
                pltpu.make_async_copy(
                    land.at[c, :, piece], ref.at[:, piece], write_sem.at[c * pieces + i]
                )
            )
    for copy in copies:
        copy.start()
    for copy in copies:
        copy.wait()


def body(queries, keys, values, grad_out, rates, doc_lengths):
    length, columns = queries.shape
    heads = rates.shape[0]
    head_dim = columns // heads
    shards = lax.axis_size("seq")
    groups = lax.axis_size("head")
    part = length // groups
    docs = doc_lengths.shape[0]
    hbm = pl.BlockSpec(memory_space=pltpu.HBM)
    vmem = pl.BlockSpec(memory_space=pltpu.VMEM)
    bf16, f32 = jnp.bfloat16, jnp.float32
    landed = pl.pallas_call(
        functools.partial(kernel, shards, groups, docs),
        out_shape=pltpu.VMEM((3, part, groups * columns), bf16),
        in_specs=[hbm] * 6,
        out_specs=vmem,
        scratch_shapes=[
            pltpu.SMEM(doc_lengths.shape, jnp.int32),
            pltpu.SMEM(rates.shape, f32),
            pltpu.VMEM((heads, 4, length, head_dim), bf16),
            pltpu.VMEM((length, length), f32),
            pltpu.VMEM((4, length, head_dim), f32),
            pltpu.VMEM((heads, 2, head_dim, head_dim), f32),
            pltpu.VMEM((heads, 2, head_dim, head_dim), f32),
            pltpu.VMEM((heads, 2, head_dim // 2, head_dim), f32),
            pltpu.VMEM((heads, shards // 2 - 1, 2, head_dim // 2, head_dim), f32),
            pltpu.VMEM((3, length, head_dim), f32),
            pltpu.VMEM((heads, groups, 3, part, head_dim), bf16),
            pltpu.SMEM((2, shards // 2 + 2), f32),
            pltpu.SemaphoreType.DMA((heads,)),
            pltpu.SemaphoreType.DMA,
            pltpu.SemaphoreType.DMA((heads,)),
            pltpu.SemaphoreType.DMA,
            pltpu.SemaphoreType.DMA((heads,)),
            pltpu.SemaphoreType.DMA,
            pltpu.SemaphoreType.DMA((groups - 1, heads)),
            pltpu.SemaphoreType.DMA((2,)),
        ],
        compiler_params=pltpu.CompilerParams(
            collective_id=0, has_side_effects=True, vmem_limit_bytes=VMEM_BYTES - 6 * part * groups * columns
        ),
        cost_estimate=pl.CostEstimate(
            flops=heads * length * (10 * length + 10 * head_dim) * head_dim,
            bytes_accessed=7 * length * columns * 2,
            transcendentals=heads * length * (length + 4 * head_dim),
        ),
    )(doc_lengths, rates, queries, keys, values, grad_out)
    out = jax.ShapeDtypeStruct((part, groups * columns), bf16)
    return pl.pallas_call(
        write_out,
        out_shape=(out, out, out),
        in_specs=[pl.BlockSpec(memory_space=pl.ANY)],
        out_specs=(hbm, hbm, hbm),
        scratch_shapes=[pltpu.SemaphoreType.DMA((12,))],
        compiler_params=pltpu.CompilerParams(vmem_limit_bytes=1024 * 1024),
    )(landed)


def solution(mesh):
    return jax.shard_map(
        body,
        mesh=mesh,
        in_specs=(
            P("seq", "head"),
            P("seq", "head"),
            P("seq", "head"),
            P("seq", "head"),
            P("head"),
            P(),
        ),
        out_specs=(P(("seq", "head"), None), P(("seq", "head"), None), P(("seq", "head"), None)),
        check_vma=False,
    )
```
